256 devices in a mesh: row: 32 (over z, x_lo, core), blk: 8 (over x_hi, y).
Axes of the slice: x: 4 (x_hi: 2, x_lo: 2; x = x_hi * 2 + x_lo), y: 4, z: 8, core: 2. Of those that a mesh axis runs over, the one named last changes fastest.
Arguments:
- features: bfloat16 [32768, 256], P(('row', 'blk')), may hold values from -6 to 6
- grad_out: bfloat16 [32768, 256], P(('row', 'blk')), may hold values from -6 to 6
- w_self: bfloat16 [256, 256], replicated, may hold values from -0.375 to 0.375
- w_neigh: bfloat16 [256, 256], replicated, may hold values from -0.375 to 0.375
- tiles: bfloat16 [256, 192, 128, 128], P(('row', 'blk')), may hold values from 0 to 1
- tile_rows: int32 [256, 192], P(('row', 'blk')), may hold values from 0 to 7, as said below
- tile_cols: int32 [256, 192], P(('row', 'blk')), may hold values from 0 to 31, as said below
- tile_counts: int32 [256], P(('row', 'blk')), may hold values from 32 to 192, as said below
- degrees: int32 [32768], P(('row', 'blk')), may hold values from 8 to 127
Outputs:
- grad_x: bfloat16 [32768, 256], P(('row', 'blk'))
- grad_w_self: float32 [256, 256], replicated
- grad_w_neigh: float32 [256, 256], replicated
The draws below stay inside these ranges and needn't reach their ends.
Inputs may be any that keep to these rules, and one draw needn't show every extreme that they name: `tile_counts`: live tile slots of each device; some device is full in every draw. `tile_rows`: the first 8 slots of each device name every row tile once. `tile_cols`: the first 32 slots of each device name every column tile once.
All inputs are finite; a program needn't handle non-finite values.
Results may differ from the reference program's by a relative error of at most 0.0046.
Values may be sent and summed in bfloat16 or wider, within the bound.
No kernel may reach another device: no remote copies, remote signals or barrier semaphores. Data moves between devices by JAX's collectives and lax.ppermute only.
A program may use at most 128 MiB of HBM per device.

```python
import jax
import jax.numpy as jnp
from jax import lax

WIDTH = 256
TILE = 128
SPAN = 128
TCAP = 192
NDEV = 256
NODES = 32768
ROW_TILES = 8
COL_TILES = 32
N_ROW = 32
N_BLK = 8


def draw_tile_counts(key, part):
    key = jax.random.fold_in(key, 1)
    first, second, third = jax.random.split(key, 3)
    lower = jax.random.randint(first, (NDEV,), COL_TILES, TCAP + 1)
    other = jax.random.randint(second, (NDEV,), COL_TILES, TCAP + 1)
    counts = jnp.minimum(lower, other)
    fullest = jax.random.randint(third, (), 0, NDEV)
    return jnp.where(jnp.arange(NDEV) == fullest, TCAP, counts).astype(jnp.int32)


def draw_tile_rows(key, part):
    key = jax.random.fold_in(key, 2)
    first, second = jax.random.split(key, 2)
    slots = jnp.arange(TCAP)[None, :]
    random_rows = jax.random.randint(first, (NDEV, TCAP), 0, ROW_TILES)
    offsets = jax.random.randint(second, (NDEV, 1), 0, ROW_TILES)
    return jnp.where(slots < ROW_TILES, (slots + offsets) % ROW_TILES, random_rows).astype(jnp.int32)


def draw_tile_cols(key, part):
    key = jax.random.fold_in(key, 3)
    first, second = jax.random.split(key, 2)
    slots = jnp.arange(TCAP)[None, :]
    random_cols = jax.random.randint(first, (NDEV, TCAP), 0, COL_TILES)
    offsets = jax.random.randint(second, (NDEV, 1), 0, COL_TILES)
    return jnp.where(slots < COL_TILES, (slots + offsets) % COL_TILES, random_cols).astype(jnp.int32)


def set_ends(values, rng, low, high):
    longest = values.shape.index(max(values.shape))
    spots = []
    for shift in (0, 1):
        where = [jax.random.randint(jax.random.fold_in(rng, axis), (), 0, length) for axis, length in enumerate(values.shape)]
        where[longest] = (where[longest] + shift) % values.shape[longest]
        spots.append(tuple(where))
    return values.at[spots[0]].set(low).at[spots[1]].set(high)


def steps_of(rng, shape, shards, low, largest):
    level = 1.0
    for dim, shards_of in shards:
        steps = jax.random.uniform(jax.random.fold_in(jax.random.fold_in(rng, 6), dim), (shards_of,), jnp.float32, low / len(shards), largest / len(shards))
        level = level * jnp.repeat(jnp.exp(steps), shape[dim] // shards_of).reshape((-1,) + (1,) * (len(shape) - 1 - dim))
    return level


def normal_values(key, extent, scale, reach, cuts=(), kind=jnp.bfloat16):
    result = jax.random.normal(key, extent, jnp.float32) * scale
    if len(cuts) > 0:
        result = steps_of(key, extent, cuts, -0.22, 0.18) * result
    return jnp.clip(result, min=-reach, max=reach).astype(kind)


def setup_inputs(seed: int = 0) -> dict:
    key_of = jax.random.split(jax.random.key(seed), 10)
    features = normal_values(key_of[0], (NODES, WIDTH), 1.0, 6.0, ((0, 256),))
    grad_out = normal_values(key_of[1], (NODES, WIDTH), 1.0, 6.0, ((0, 256),))
    w_self = normal_values(key_of[2], (WIDTH, WIDTH), WIDTH ** -0.5, 0.375)
    w_neigh = normal_values(key_of[3], (WIDTH, WIDTH), WIDTH ** -0.5, 0.375)
    tiles = jnp.clip(1.0 * jax.random.uniform(key_of[4], (NDEV, TCAP, TILE, TILE), jnp.float32) ** steps_of(key_of[4], (NDEV, TCAP, TILE, TILE), ((0, 256),), -0.2, 0.2), 0.0, 1.0).astype(jnp.bfloat16)
    tile_rows = draw_tile_rows(jax.random.fold_in(key_of[9], 71), 0)
    tile_cols = draw_tile_cols(jax.random.fold_in(key_of[9], 71), 0)
    tile_counts = draw_tile_counts(jax.random.fold_in(key_of[9], 71), 0)
    degrees = set_ends(jax.random.randint(key_of[8], (NODES,), 8, 128), jax.random.fold_in(key_of[8], 1), 8, 127).astype(jnp.int32)
    return {"features": features, "grad_out": grad_out, "w_self": w_self, "w_neigh": w_neigh, "tiles": tiles, "tile_rows": tile_rows, "tile_cols": tile_cols, "tile_counts": tile_counts, "degrees": degrees}


def reference(features, grad_out, w_self, w_neigh, tiles, tile_rows, tile_cols, tile_counts, degrees):
    highest = lax.Precision.HIGHEST
    degree_f = degrees.astype(jnp.float32)[:, None]
    dagg = jnp.dot(grad_out, w_neigh.T, preferred_element_type=jnp.float32)
    scaled = (dagg / degree_f).astype(jnp.bfloat16)
    class_all = features.reshape(N_ROW, N_BLK, SPAN, WIDTH)
    group_all = scaled.reshape(N_ROW, N_BLK * SPAN, WIDTH)
    slot_ids = jnp.arange(TCAP, dtype=jnp.int32)
    row_ids = jnp.arange(ROW_TILES, dtype=jnp.int32)
    col_ids = jnp.arange(COL_TILES, dtype=jnp.int32)

    def device_step(accums, device_index):
        agg_acc, column_acc = accums
        row_pos = device_index // N_BLK
        blk_pos = device_index % N_BLK
        class_feats = lax.dynamic_index_in_dim(class_all, blk_pos, 1, False).reshape(COL_TILES, TILE, WIDTH)
        scaled_group = lax.dynamic_index_in_dim(group_all, row_pos, 0, False).reshape(ROW_TILES, TILE, WIDTH)
        alive_mask = (slot_ids < tile_counts[device_index]).astype(jnp.float32)
        tile_block = tiles[device_index].astype(jnp.float32) * alive_mask[:, None, None]
        row_slot = tile_rows[device_index]
        col_slot = tile_cols[device_index]
        feat_tiles = class_feats[col_slot].astype(jnp.float32)
        forward_part = jnp.einsum('tij,tjf->tif', tile_block, feat_tiles, precision=highest)
        row_onehot = (row_slot[:, None] == row_ids[None, :]).astype(jnp.float32)
        agg_part = jnp.einsum('tk,tif->kif', row_onehot, forward_part, precision=highest)
        scaled_tiles = scaled_group[row_slot].astype(jnp.float32)
        backward_part = jnp.einsum('tij,tif->tjf', tile_block, scaled_tiles, precision=highest)
        col_onehot = (col_slot[:, None] == col_ids[None, :]).astype(jnp.float32)
        column_part = jnp.einsum('tk,tjf->kjf', col_onehot, backward_part, precision=highest)
        agg_acc = agg_acc.at[row_pos].add(agg_part.reshape(N_BLK * SPAN, WIDTH))
        column_acc = column_acc.at[blk_pos].add(column_part.reshape(N_ROW * SPAN, WIDTH))
        return (agg_acc, column_acc), None

    start = (jnp.zeros((N_ROW, N_BLK * SPAN, WIDTH), jnp.float32), jnp.zeros((N_BLK, N_ROW * SPAN, WIDTH), jnp.float32))
    (agg_acc, column_acc), _ = lax.scan(device_step, start, jnp.arange(N_ROW * N_BLK, dtype=jnp.int32))
    agg = agg_acc.reshape(NODES, WIDTH) / degree_f
    column_sum = column_acc.reshape(N_BLK, N_ROW, SPAN, WIDTH).transpose(1, 0, 2, 3).reshape(NODES, WIDTH)
    grad_x = (jnp.dot(grad_out, w_self.T, preferred_element_type=jnp.float32) + column_sum).astype(jnp.bfloat16)
    grad_w_self = jnp.dot(features.T, grad_out, preferred_element_type=jnp.float32) / NODES
    grad_w_neigh = jnp.dot(agg.T, grad_out.astype(jnp.float32), precision=highest) / NODES
    return grad_x, grad_w_self, grad_w_neigh
```

```python
import itertools

import jax
import jax.numpy as jnp
from jax import lax
from jax.experimental import pallas as pl
from jax.experimental.pallas import tpu as pltpu
from jax.sharding import PartitionSpec as P

PARTS = {"z": 8, "xl": 2, "core": 2, "xh": 2, "y": 4}
CHUNK = 16
DEG_ROWS = 16


def device_id(where):
    row = (where["z"] * 2 + where["xl"]) * 2 + where["core"]
    return row * 8 + where["xh"] * 4 + where["y"]


def groups_of(names):
    rest = [name for name in PARTS if name not in names]
    groups = []
    for fixed in itertools.product(*[range(PARTS[name]) for name in rest]):
        where = dict(zip(rest, fixed))
        group = []
        for moving in itertools.product(*[range(PARTS[name]) for name in names]):
            where.update(zip(names, moving))
            group.append(device_id(where))
        groups.append(group)
    return groups


def exchange(blocks, names):
    return lax.all_to_all(
        blocks, ("row", "blk"), 0, 0, axis_index_groups=groups_of(names), tiled=True
    )


def spread(block, names, count):
    return exchange(jnp.broadcast_to(block[None], (count,) + block.shape), names)


def swap_core(value):
    return lax.ppermute(value, "row", [(row, row ^ 1) for row in range(32)])


def sparse_kernel(rows, cols, meta, grads, tiles, mine, theirs, acc, lhs):
    step = pl.program_id(0)
    live = meta[0]
    core = meta[1]

    @pl.when(step == 0)
    def _():
        for k in range(8):
            grad_t = grads[k, 0:128, :].T.astype(jnp.float32)
            degree = grads[k, 128:129, 0:128].astype(jnp.float32)
            value = grad_t / degree
            high = value.astype(jnp.bfloat16)
            low = (value - high.astype(jnp.float32)).astype(jnp.bfloat16)
            lhs[k, :, 0:128] = high
            lhs[k, :, 128:256] = low
        lhs[8] = jnp.zeros((256, 256), jnp.bfloat16)
        for k in range(32):
            acc[k] = jnp.zeros((256, 128), jnp.float32)

    @pl.when(step * CHUNK < live)
    def _():
        for u in range(CHUNK):
            slot = step * CHUNK + u
            row = jnp.where(slot < live, rows[slot], 8)
            col = cols[slot]
            tile = tiles[u]
            product = jnp.dot(
                lhs[row],
                jnp.concatenate([tile, tile], axis=0),
                preferred_element_type=jnp.float32,
            )
            acc[col] += product

    @pl.when(step == pl.num_programs(0) - 1)
    def _():
        def move(k, carry):
            mine[k] = acc[2 * k + core]
            theirs[k] = acc[2 * k + 1 - core].astype(jnp.bfloat16)
            return carry

        lax.fori_loop(0, 16, move, 0)


def sparse_product(rows, cols, meta, grads, tiles):
    steps = tiles.shape[0] // CHUNK

    def tile_block(i, rows, cols, meta):
        return (jnp.minimum(i, (meta[0] - 1) // CHUNK), 0, 0)

    whole = lambda i, rows, cols, meta: (0, 0, 0)
    return pl.pallas_call(
        sparse_kernel,
        grid_spec=pltpu.PrefetchScalarGridSpec(
            num_scalar_prefetch=3,
            grid=(steps,),
            in_specs=[
                pl.BlockSpec(grads.shape, whole),
                pl.BlockSpec((CHUNK, 128, 128), tile_block),
            ],
            out_specs=[
                pl.BlockSpec((16, 256, 128), whole),
                pl.BlockSpec((16, 256, 128), whole),
            ],
            scratch_shapes=[
                pltpu.VMEM((32, 256, 128), jnp.float32),
                pltpu.VMEM((9, 256, 256), jnp.bfloat16),
            ],
        ),
        out_shape=[
            jax.ShapeDtypeStruct((16, 256, 128), jnp.float32),
            jax.ShapeDtypeStruct((16, 256, 128), jnp.bfloat16),
        ],
        compiler_params=pltpu.CompilerParams(vmem_limit_bytes=40 * 1024 * 1024),
        name="sparse",
    )(rows, cols, meta, grads, tiles)


def dense_kernel(parts, feats, grads, w_self, w_neigh, grad_x, grad_neigh):
    total = parts[0].astype(jnp.float32)
    for k in range(1, 16):
        total += parts[k].astype(jnp.float32)
    high = total.astype(jnp.bfloat16)
    low = (total - high.astype(jnp.float32)).astype(jnp.bfloat16)
    feat = feats[...]
    neigh_t = jnp.dot(
        jnp.concatenate([high, low], axis=1),
        jnp.concatenate([feat, feat], axis=0),
        preferred_element_type=jnp.float32,
    )
    grad_neigh[...] = neigh_t.T
    nt = (((1,), (1,)), ((), ()))
    out = lax.dot_general(w_self[...], grads[...], nt, preferred_element_type=jnp.float32)
    out += jnp.dot(w_neigh[...], high, preferred_element_type=jnp.float32)
    out += jnp.dot(w_neigh[...], low, preferred_element_type=jnp.float32)
    grad_x[...] = out.T.astype(jnp.bfloat16)


def dense_part(parts, feats, grads, w_self, w_neigh):
    return pl.pallas_call(
        dense_kernel,
        out_shape=[
            jax.ShapeDtypeStruct((128, 256), jnp.bfloat16),
            jax.ShapeDtypeStruct((256, 256), jnp.float32),
        ],
        compiler_params=pltpu.CompilerParams(vmem_limit_bytes=32 * 1024 * 1024),
        name="dense",
    )(parts, feats, grads, w_self, w_neigh)


def shards(features, grad_out, w_self, w_neigh, tiles, tile_rows, tile_cols, tile_counts, degrees):
    core = lax.axis_index("row") & 1
    node_total = 128 * 256
    degree_rows = jnp.pad(degrees.astype(jnp.bfloat16)[None], ((0, DEG_ROWS - 1), (0, 128)))
    packed = jnp.concatenate([grad_out, degree_rows], axis=0)
    group = spread(packed, ("xh", "y"), 8)
    meta = jnp.stack([tile_counts[0], core.astype(jnp.int32)])
    mine, theirs = sparse_product(tile_rows[0], tile_cols[0], meta, group, tiles[0])
    halves = (mine + swap_core(theirs).astype(jnp.float32)).astype(jnp.bfloat16)
    parts = exchange(halves, ("z", "xl"))
    grad_x, neigh = dense_part(parts, features, grad_out, w_self, w_neigh)
    own = jnp.einsum("nf,ng->fg", features, grad_out, preferred_element_type=jnp.float32)
    first = core == 0
    kept = jnp.where(first, own, neigh) + swap_core(jnp.where(first, neigh, own))
    pieces = exchange(kept.reshape(16, 16, 256), ("xh", "xl", "y")).sum(axis=0)
    pieces = spread(pieces, ("z",), 8).sum(axis=0) / node_total
    full = spread(pieces, ("xh", "xl", "y"), 16).reshape(256, 256)
    other = swap_core(full)
    return grad_x, jnp.where(first, full, other), jnp.where(first, other, full)


def solution(mesh):
    in_specs = (
        P(("row", "blk"), None),
        P(("row", "blk"), None),
        P(),
        P(),
        P(("row", "blk"), None, None, None),
        P(("row", "blk"), None),
        P(("row", "blk"), None),
        P(("row", "blk")),
        P(("row", "blk")),
    )
    out_specs = (P(("row", "blk"), None), P(), P())
    return jax.shard_map(shards, mesh=mesh, in_specs=in_specs, out_specs=out_specs, check_vma=False)
```

```python
import functools
import itertools

import jax
import jax.numpy as jnp
from jax import lax
from jax.experimental import pallas as pl
from jax.experimental.pallas import tpu as pltpu
from jax.sharding import PartitionSpec as P

PARTS = {"z": 8, "xl": 2, "core": 2, "xh": 2, "y": 4}
CHUNK = 16
DEG_ROWS = 16
UNROLL = 8
TRASH = 32
ZERO_ROW = 8
MIB = 1024 * 1024
SPARSE_MIB = 48
VMEM = pl.BlockSpec(memory_space=pltpu.VMEM)
SMEM = pl.BlockSpec(memory_space=pltpu.SMEM)
ANY = pl.BlockSpec(memory_space=pl.ANY)


def device_id(where):
    row = (where["z"] * 2 + where["xl"]) * 2 + where["core"]
    return row * 8 + where["xh"] * 4 + where["y"]


def groups_of(names):
    rest = [name for name in PARTS if name not in names]
    groups = []
    for fixed in itertools.product(*[range(PARTS[name]) for name in rest]):
        where = dict(zip(rest, fixed))
        group = []
        for moving in itertools.product(*[range(PARTS[name]) for name in names]):
            where.update(zip(names, moving))
            group.append(device_id(where))
        groups.append(group)
    return groups


def exchange(blocks, names):
    return lax.all_to_all(
        blocks, ("row", "blk"), 0, 0, axis_index_groups=groups_of(names), tiled=True
    )


def spread(block, names, count):
    return exchange(jnp.broadcast_to(block[None], (count,) + block.shape), names)


def swap_core(value):
    return lax.ppermute(value, "row", [(row, row ^ 1) for row in range(32)])


def params(mib):
    return pltpu.CompilerParams(vmem_limit_bytes=mib * MIB)


def head_kernel(grads, degrees, out, degree, sems):
    copies = [pltpu.make_async_copy(degrees, degree, sems.at[8])]
    for k in range(8):
        copies.append(pltpu.make_async_copy(grads, out.at[k, pl.ds(0, 128)], sems.at[k]))
    for copy in copies:
        copy.start()
    copies[0].wait()
    value = jnp.broadcast_to(degree[...], (DEG_ROWS, 128)).astype(jnp.float32)
    for k in range(8):
        out[k, 128 : 128 + DEG_ROWS, 0:128] = value.astype(jnp.bfloat16)
        out[k, 128 : 128 + DEG_ROWS, 128:256] = jnp.zeros((DEG_ROWS, 128), jnp.bfloat16)
    for copy in copies[1:]:
        copy.wait()


def head(grads, degrees):
    return pl.pallas_call(
        head_kernel,
        in_specs=[ANY, ANY],
        out_specs=VMEM,
        out_shape=jax.ShapeDtypeStruct((8, 128 + DEG_ROWS, 256), jnp.bfloat16),
        scratch_shapes=[pltpu.VMEM((1, 128), jnp.int32), pltpu.SemaphoreType.DMA((9,))],
        compiler_params=params(60),
        name="head",
    )(grads, degrees[None])


def prep_kernel(counts, row, rows, cols, feats, grads, plan, own_self):
    own_self[...] = lax.dot_general(
        feats[...], grads[...], (((0,), (0,)), ((), ())), preferred_element_type=jnp.float32
    )
    live = counts[0]
    slots = rows.shape[1]
    narrow = lambda value: value.astype(jnp.float32).astype(jnp.bfloat16)
    slot = lax.broadcasted_iota(jnp.int32, (1, slots), 1)
    lanes = lax.broadcasted_iota(jnp.int32, (8, slots), 0)
    hot = jnp.where((rows[...] == lanes) & (slot < live), 1.0, 0.0)
    earlier = lax.broadcasted_iota(jnp.int32, (slots, slots), 0) < lax.broadcasted_iota(
        jnp.int32, (slots, slots), 1
    )
    rank = jnp.dot(
        hot.astype(jnp.bfloat16),
        jnp.where(earlier, 1.0, 0.0).astype(jnp.bfloat16),
        preferred_element_type=jnp.float32,
    )
    rank = jnp.sum(hot * rank, axis=0, keepdims=True).astype(jnp.int32)
    pairs = (jnp.sum(hot, axis=1, keepdims=True).astype(jnp.int32) + 1) >> 1
    start = jnp.zeros((8, 1), jnp.int32)
    for r in range(7):
        start += jnp.where(lax.broadcasted_iota(jnp.int32, (8, 1), 0) > r, pairs[r : r + 1], 0)
    total = start[7:8] + pairs[7:8]
    start = jnp.sum(hot * start.astype(jnp.float32), axis=0, keepdims=True).astype(jnp.int32)
    pair = jnp.where(slot < live, start + (rank >> 1), -1)
    far = cols[...] ^ row[0]
    place = (far & 1) * 16 + (far & 4) * 2 + (far & 8) // 2 + (far & 2) + (far >> 4)
    values = jnp.where(lanes == 0, slot, 0) + jnp.where(lanes == 1, place, 0)
    values += jnp.where(lanes == 2, rows[...], 0) + jnp.where(lanes == 3, 1, 0)
    mine = lax.broadcasted_iota(jnp.int32, (128, slots), 0) == pair
    nt = (((1,), (1,)), ((), ()))

    def pick(half):
        chosen = jnp.where(mine & ((rank & 1) == half), 1.0, 0.0).astype(jnp.bfloat16)
        picked = lax.dot_general(narrow(values), chosen, nt, preferred_element_type=jnp.float32)
        return picked.astype(jnp.int32)

    first, second = pick(0), pick(1)
    plan[0:1, :] = first[0:1]
    plan[1:2, :] = second[0:1]
    plan[2:3, :] = first[1:2] + (1 - first[3:4]) * TRASH
    plan[3:4, :] = second[1:2] + (1 - second[3:4]) * TRASH
    plan[4:5, :] = first[2:3] + (1 - first[3:4]) * ZERO_ROW
    plan[5:6, :] = jnp.broadcast_to((total + UNROLL - 1) >> 3, (1, 128))
    plan[6:7, :] = jnp.full((1, 128), (live + CHUNK - 1) >> 4, jnp.int32)
    plan[7:8, :] = jnp.zeros((1, 128), jnp.int32)


def prep(counts, row, rows, cols, feats, grads):
    return pl.pallas_call(
        prep_kernel,
        in_specs=[SMEM, SMEM, VMEM, VMEM, VMEM, VMEM],
        out_specs=[VMEM, VMEM],
        out_shape=[
            jax.ShapeDtypeStruct((8, 128), jnp.int32),
            jax.ShapeDtypeStruct((256, 256), jnp.float32),
        ],
        compiler_params=params(10),
        cost_estimate=pl.CostEstimate(flops=0, bytes_accessed=4 * MIB, transcendentals=0),
        name="prep",
    )(counts, row[None], rows, cols, feats, grads)


def join_kernel(first, second, out):
    out[0 : first.shape[0]] = first[...]
    out[first.shape[0] :] = second[...]


def join(first, second):
    return pl.pallas_call(
        join_kernel,
        in_specs=[VMEM, VMEM],
        out_specs=VMEM,
        out_shape=jax.ShapeDtypeStruct((2 * first.shape[0],) + first.shape[1:], first.dtype),
        compiler_params=params(4),
        name="join",
    )(first, second)


def sparse_kernel(plan, grads, tiles, near, away, near_out, away_out, lhs, acc, held, sems):
    chunks = plan[6, 0]

    def piece(k):
        part = pl.ds(k * CHUNK, CHUNK)
        return pltpu.make_async_copy(tiles.at[part], held.at[part], sems.at[k])

    def wait_piece(k, carry):
        piece(k).wait()
        return carry

    for k in range(192 // CHUNK):
        pl.when(k < chunks)(lambda k=k: piece(k).start())
    for k in range(8):
        grad_t = grads[k, 0:128, :].T.astype(jnp.float32)
        degree = grads[k, 128:129, 0:128].astype(jnp.float32)
        value = grad_t / degree
        high = value.astype(jnp.bfloat16)
        low = (value - high.astype(jnp.float32)).astype(jnp.bfloat16)
        lhs[k, :, 0:128] = high
        lhs[k, :, 128:256] = low
    lhs[ZERO_ROW] = jnp.zeros((256, 256), jnp.bfloat16)

    def clear(k, carry):
        acc[k] = jnp.zeros((256, 128), jnp.float32)
        return carry

    lax.fori_loop(0, 33, clear, 0)

    lax.fori_loop(0, chunks, wait_piece, 0)

    def pairs(step, carry):
        for u in range(UNROLL):
            p = step * UNROLL + u
            both = jnp.concatenate([held[plan[0, p]], held[plan[1, p]]], axis=1)
            product = jnp.dot(
                lhs[plan[4, p]],
                jnp.concatenate([both, both], axis=0),
                preferred_element_type=jnp.float32,
            )
            acc[plan[2, p]] += product[:, 0:128]
            acc[plan[3, p]] += product[:, 128:256]
        return carry

    lax.fori_loop(0, plan[5, 0], pairs, 0)

    def move(k, carry):
        near[k] = acc[k]
        away[k] = acc[8 + k]
        near_out[k] = acc[16 + k].astype(jnp.bfloat16)
        away_out[k] = acc[24 + k].astype(jnp.bfloat16)
        return carry

    lax.fori_loop(0, 8, move, 0)


def sparse_product(plan, grads, tiles):
    return pl.pallas_call(
        sparse_kernel,
        in_specs=[SMEM, VMEM, pl.BlockSpec(memory_space=pl.ANY)],
        out_specs=[VMEM] * 4,
        out_shape=[
            jax.ShapeDtypeStruct((8, 256, 128), kind)
            for kind in (jnp.float32, jnp.float32, jnp.bfloat16, jnp.bfloat16)
        ],
        scratch_shapes=[
            pltpu.VMEM((9, 256, 256), jnp.bfloat16),
            pltpu.VMEM((33, 256, 128), jnp.float32),
            pltpu.VMEM((192, 128, 128), jnp.bfloat16),
            pltpu.SemaphoreType.DMA((192 // CHUNK,)),
        ],
        compiler_params=params(SPARSE_MIB),
        cost_estimate=pl.CostEstimate(flops=4 * 10**9, bytes_accessed=12 * MIB, transcendentals=0),
        name="sparse",
    )(plan, grads, tiles)


def neigh_kernel(core, near, core_part, x_part, feats_low, feats_high, own_self, keep, send, kept, sent):
    total_t = jnp.zeros((256, 256), jnp.float32)
    for k in range(8):
        block = near[k] + core_part[k].astype(jnp.float32) + x_part[k].astype(jnp.float32)
        high = block.astype(jnp.bfloat16)
        low = (block - high.astype(jnp.float32)).astype(jnp.bfloat16)
        if k < 4:
            keep[k] = block
        else:
            send[k - 4] = high
        feat = (feats_high if k & 2 else feats_low)[(k & 1) * 2 + (k >> 2)]
        total_t += jnp.dot(
            jnp.concatenate([high, low], axis=1),
            jnp.concatenate([feat, feat], axis=0),
            preferred_element_type=jnp.float32,
        )
    total = total_t.T
    first = core[0] == 0

    @pl.when(first)
    def _():
        kept[...] = own_self[...]
        sent[...] = total

    @pl.when(jnp.logical_not(first))
    def _():
        kept[...] = total
        sent[...] = own_self[...]


def neigh_part(core, near, core_part, x_part, feats_low, feats_high, own_self):
    return pl.pallas_call(
        neigh_kernel,
        in_specs=[SMEM] + [VMEM] * 6,
        out_specs=[VMEM] * 4,
        out_shape=[
            jax.ShapeDtypeStruct((4, 256, 128), jnp.float32),
            jax.ShapeDtypeStruct((4, 256, 128), jnp.bfloat16),
            jax.ShapeDtypeStruct((256, 256), jnp.float32),
            jax.ShapeDtypeStruct((256, 256), jnp.float32),
        ],
        compiler_params=params(16),
        cost_estimate=pl.CostEstimate(flops=10**9, bytes_accessed=4 * MIB, transcendentals=0),
        name="neigh",
    )(core[None], near, core_part, x_part, feats_low, feats_high, own_self)


def fold_kernel(scale, pieces, keep, got, out, *rest):
    total = pieces[0]
    for k in range(1, pieces.shape[0]):
        total += pieces[k]
    total = total * scale
    for k in range(out.shape[0]):
        out[k] = total
    half = keep.shape[0] // 2
    kept, send = rest
    for k in range(half):
        kept[k] = keep[k] + got[k].astype(jnp.float32)
        send[k] = (keep[half + k] + got[half + k].astype(jnp.float32)).astype(jnp.bfloat16)


def fold(scale, pieces, receivers, keep, got):
    half = keep.shape[0] // 2
    return pl.pallas_call(
        functools.partial(fold_kernel, scale),
        in_specs=[VMEM] * 3,
        out_specs=[VMEM] * 3,
        out_shape=[
            jax.ShapeDtypeStruct((receivers, 16, 256), jnp.float32),
            jax.ShapeDtypeStruct((half, 256, 128), jnp.float32),
            jax.ShapeDtypeStruct((half, 256, 128), jnp.bfloat16),
        ],
        compiler_params=params(8),
        name="fold",
    )(pieces, keep, got)


def last_kernel(core, own, part, grads, w_self, w_neigh, full, other, grad_x, grad_self, grad_neigh):
    first = core[0] == 0

    @pl.when(first)
    def _():
        grad_self[...] = full[...]
        grad_neigh[...] = other[...]

    @pl.when(jnp.logical_not(first))
    def _():
        grad_self[...] = other[...]
        grad_neigh[...] = full[...]

    total = own[0] + part[0].astype(jnp.float32)
    high = total.astype(jnp.bfloat16)
    low = (total - high.astype(jnp.float32)).astype(jnp.bfloat16)
    nt = (((1,), (1,)), ((), ()))
    out = lax.dot_general(w_self[...], grads[...], nt, preferred_element_type=jnp.float32)
    out += jnp.dot(w_neigh[...], high, preferred_element_type=jnp.float32)
    out += jnp.dot(w_neigh[...], low, preferred_element_type=jnp.float32)
    grad_x[...] = out.T.astype(jnp.bfloat16)


def last(core, own, part, grads, w_self, w_neigh, full, other):
    return pl.pallas_call(
        last_kernel,
        in_specs=[SMEM] + [VMEM] * 7,
        out_specs=[VMEM] * 3,
        out_shape=[
            jax.ShapeDtypeStruct((128, 256), jnp.bfloat16),
            jax.ShapeDtypeStruct((256, 256), jnp.float32),
            jax.ShapeDtypeStruct((256, 256), jnp.float32),
        ],
        compiler_params=params(8),
        name="last",
    )(core[None], own, part, grads, w_self, w_neigh, full, other)


def swap_z(value, distance):
    return lax.ppermute(value, "row", [(row, row ^ (4 * distance)) for row in range(32)])


def swap_x(value):
    return lax.ppermute(value, "row", [(row, row ^ 2) for row in range(32)])


def shards(features, grad_out, w_self, w_neigh, tiles, tile_rows, tile_cols, tile_counts, degrees):
    row = lax.axis_index("row").astype(jnp.int32)
    core = row & 1
    node_total = 128 * 256
    group = exchange(head(grad_out, degrees), ("xh", "y"))
    plan, own_self = prep(tile_counts, row, tile_rows, tile_cols, features, grad_out)
    feats = features[None]
    feats = join(feats, swap_z(feats, 2))
    feats_far = swap_z(feats, 4)
    group, feats, plan = lax.optimization_barrier((group, feats, plan))
    near, away, near_out, away_out = sparse_product(plan, group, tiles[0])
    away_out, feats_far = lax.optimization_barrier((away_out, feats_far))
    feats = join(feats, feats_far)
    away = (away + swap_core(away_out).astype(jnp.float32)).astype(jnp.bfloat16)
    core_part = swap_core(near_out)
    z_part = swap_z(away, 1)
    feats_x = swap_x(feats)
    keep, send, kept, sent = neigh_part(core, near, core_part, z_part, feats, feats_x, own_self)
    kept = kept + swap_core(sent)
    got = swap_z(send, 2)
    pieces = exchange(kept.reshape(16, 16, 256), ("xh", "xl", "y"))
    pieces, keep, send = fold(1.0, pieces, 8, keep, got)
    got = swap_x(send)
    pieces = exchange(pieces, ("z",))
    pieces, keep, send = fold(1.0 / node_total, pieces, 16, keep, got)
    got = swap_z(send, 4)
    full = exchange(pieces, ("xh", "xl", "y")).reshape(256, 256)
    full, got = lax.optimization_barrier((full, got))
    other = swap_core(full)
    return last(core, keep, got, grad_out, w_self, w_neigh, full, other)


def solution(mesh):
    in_specs = (
        P(("row", "blk"), None),
        P(("row", "blk"), None),
        P(),
        P(),
        P(("row", "blk"), None, None, None),
        P(("row", "blk"), None),
        P(("row", "blk"), None),
        P(("row", "blk")),
        P(("row", "blk")),
    )
    out_specs = (P(("row", "blk"), None), P(), P())
    return jax.shard_map(shards, mesh=mesh, in_specs=in_specs, out_specs=out_specs, check_vma=False)
```

```python
import functools
import itertools

import jax
import jax.numpy as jnp
from jax import lax
from jax.experimental import pallas as pl
from jax.experimental.pallas import tpu as pltpu
from jax.sharding import PartitionSpec as P

PARTS = {"z": 8, "xl": 2, "core": 2, "xh": 2, "y": 4}
CHUNK = 16
DEG_ROWS = 16
UNROLL = 8
TRASH = 32
ZERO_ROW = 8
MIB = 1024 * 1024
SPARSE_MIB = 48
VMEM = pl.BlockSpec(memory_space=pltpu.VMEM)
SMEM = pl.BlockSpec(memory_space=pltpu.SMEM)
ANY = pl.BlockSpec(memory_space=pl.ANY)


def device_id(where):
    row = (where["z"] * 2 + where["xl"]) * 2 + where["core"]
    return row * 8 + where["xh"] * 4 + where["y"]


def groups_of(names):
    rest = [name for name in PARTS if name not in names]
    groups = []
    for fixed in itertools.product(*[range(PARTS[name]) for name in rest]):
        where = dict(zip(rest, fixed))
        group = []
        for moving in itertools.product(*[range(PARTS[name]) for name in names]):
            where.update(zip(names, moving))
            group.append(device_id(where))
        groups.append(group)
    return groups


def exchange(blocks, names):
    return lax.all_to_all(
        blocks, ("row", "blk"), 0, 0, axis_index_groups=groups_of(names), tiled=True
    )


def spread(block, names, count):
    return exchange(jnp.broadcast_to(block[None], (count,) + block.shape), names)


def swap_core(value):
    return lax.ppermute(value, "row", [(row, row ^ 1) for row in range(32)])


def params(mib):
    return pltpu.CompilerParams(vmem_limit_bytes=mib * MIB)


def head_kernel(grads, degrees, out, degree, sems):
    copies = [pltpu.make_async_copy(degrees, degree, sems.at[8])]
    for k in range(8):
        copies.append(pltpu.make_async_copy(grads, out.at[k, pl.ds(0, 128)], sems.at[k]))
    for copy in copies:
        copy.start()
    copies[0].wait()
    value = jnp.broadcast_to(degree[...], (DEG_ROWS, 128)).astype(jnp.float32)
    for k in range(8):
        out[k, 128 : 128 + DEG_ROWS, 0:128] = value.astype(jnp.bfloat16)
        out[k, 128 : 128 + DEG_ROWS, 128:256] = jnp.zeros((DEG_ROWS, 128), jnp.bfloat16)
    for copy in copies[1:]:
        copy.wait()


def head(grads, degrees):
    return pl.pallas_call(
        head_kernel,
        in_specs=[ANY, ANY],
        out_specs=VMEM,
        out_shape=jax.ShapeDtypeStruct((8, 128 + DEG_ROWS, 256), jnp.bfloat16),
        scratch_shapes=[pltpu.VMEM((1, 128), jnp.int32), pltpu.SemaphoreType.DMA((9,))],
        compiler_params=params(60),
        name="head",
    )(grads, degrees[None])


def prep_kernel(counts, row, rows, cols, feats, grads, plan, own_self):
    own_self[...] = lax.dot_general(
        feats[...], grads[...], (((0,), (0,)), ((), ())), preferred_element_type=jnp.float32
    )
    live = counts[0]
    slots = rows.shape[1]
    slot = lax.broadcasted_iota(jnp.int32, (1, slots), 1)
    lanes = lax.broadcasted_iota(jnp.int32, (8, slots), 0)
    hot = jnp.where((rows[...] == lanes) & (slot < live), 1.0, 0.0)
    earlier = lax.broadcasted_iota(jnp.int32, (slots, slots), 0) < lax.broadcasted_iota(
        jnp.int32, (slots, slots), 1
    )
    earlier = jnp.where(earlier, 1.0, 0.0).astype(jnp.bfloat16)

    def before(flags):
        return jnp.dot(flags.astype(jnp.bfloat16), earlier, preferred_element_type=jnp.float32)

    rank = jnp.sum(hot * before(hot), axis=0, keepdims=True).astype(jnp.int32)
    count = jnp.sum(hot * jnp.sum(hot, axis=1, keepdims=True), axis=0, keepdims=True)
    second = jnp.where((slot < live) & ((rank & 1) == 1), 1.0, 0.0)
    single = jnp.where((slot < live) & ((rank & 1) == 0) & (rank + 1 == count.astype(jnp.int32)), 1.0, 0.0)
    pairs = jnp.sum(second, axis=1, keepdims=True).astype(jnp.int32)
    total = pairs + jnp.sum(single, axis=1, keepdims=True).astype(jnp.int32)
    place_of_second = jnp.where(second > 0, before(jnp.broadcast_to(second, (8, slots)))[0:1], -1.0)
    place_of_single = before(jnp.broadcast_to(single, (8, slots)))[0:1].astype(jnp.int32) + pairs
    place_of_single = jnp.where(single > 0, place_of_single, -1)
    key = jnp.where(slot < live, rows[...] * 256 + (rank >> 1), -1).astype(jnp.float32)
    entry = lax.broadcasted_iota(jnp.int32, (128, slots), 0)
    is_second = jnp.where(entry == place_of_second.astype(jnp.int32), 1.0, 0.0)
    entry_key = jnp.sum(is_second * key, axis=1, keepdims=True)
    is_first = (entry < pairs) & (key == entry_key) & (second == 0)
    is_first = jnp.where(is_first | (entry == place_of_single), 1.0, 0.0)
    far = cols[...] ^ row[0]
    place = (far & 1) * 16 + (far & 4) * 2 + (far & 8) // 2 + (far & 2) + (far >> 4)
    values = jnp.where(lanes == 0, slot, 0) + jnp.where(lanes == 1, place, 0)
    values += jnp.where(lanes == 2, rows[...], 0) + jnp.where(lanes == 3, 1, 0)
    values = values.astype(jnp.float32).astype(jnp.bfloat16)

    def pick(chosen):
        nt = (((1,), (1,)), ((), ()))
        chosen = chosen.astype(jnp.bfloat16)
        return lax.dot_general(values, chosen, nt, preferred_element_type=jnp.float32).astype(jnp.int32)

    one, two = pick(is_first), pick(is_second)
    plan[0:1, :] = one[0:1]
    plan[1:2, :] = two[0:1]
    plan[2:3, :] = one[1:2] + (1 - one[3:4]) * TRASH
    plan[3:4, :] = two[1:2] + (1 - two[3:4]) * TRASH
    plan[4:5, :] = one[2:3] + (1 - one[3:4]) * ZERO_ROW
    plan[5:6, :] = jnp.broadcast_to((total + UNROLL - 1) >> 3, (1, 128))
    plan[6:7, :] = (jnp.maximum(one[0:1], two[0:1]) >> 4) + 1
    plan[7:8, :] = jnp.full((1, 128), (live + CHUNK - 1) >> 4, jnp.int32)


def prep(counts, row, rows, cols, feats, grads):
    return pl.pallas_call(
        prep_kernel,
        in_specs=[SMEM, SMEM, VMEM, VMEM, VMEM, VMEM],
        out_specs=[VMEM, VMEM],
        out_shape=[
            jax.ShapeDtypeStruct((8, 128), jnp.int32),
            jax.ShapeDtypeStruct((256, 256), jnp.float32),
        ],
        compiler_params=params(10),
        cost_estimate=pl.CostEstimate(flops=0, bytes_accessed=4 * MIB, transcendentals=0),
        name="prep",
    )(counts, row[None], rows, cols, feats, grads)


def join_kernel(first, second, out):
    out[0 : first.shape[0]] = first[...]
    out[first.shape[0] :] = second[...]


def join(first, second):
    return pl.pallas_call(
        join_kernel,
        in_specs=[VMEM, VMEM],
        out_specs=VMEM,
        out_shape=jax.ShapeDtypeStruct((2 * first.shape[0],) + first.shape[1:], first.dtype),
        compiler_params=params(4),
        name="join",
    )(first, second)


def sparse_kernel(plan, z, grads, tiles, near, away_a, away_b, near_out, away_out, lhs, acc, held, sems):
    chunks = plan[7, 0]

    def piece(k):
        part = pl.ds(k * CHUNK, CHUNK)
        return pltpu.make_async_copy(tiles.at[part], held.at[part], sems.at[k])

    def wait_piece(k, carry):
        piece(k).wait()
        return carry

    for k in range(192 // CHUNK):
        pl.when(k < chunks)(lambda k=k: piece(k).start())
    for k in range(8):
        grad_t = grads[k, 0:128, :].T.astype(jnp.float32)
        degree = grads[k, 128:129, 0:128].astype(jnp.float32)
        value = grad_t / degree
        high = value.astype(jnp.bfloat16)
        low = (value - high.astype(jnp.float32)).astype(jnp.bfloat16)
        lhs[k, :, 0:128] = high
        lhs[k, :, 128:256] = low
    lhs[ZERO_ROW] = jnp.zeros((256, 256), jnp.bfloat16)

    def clear(k, carry):
        acc[k] = jnp.zeros((256, 128), jnp.float32)
        return carry

    lax.fori_loop(0, 33, clear, 0)

    def pairs(step, waited):
        need = waited
        for u in range(UNROLL):
            need = jnp.maximum(need, plan[6, step * UNROLL + u])
        lax.fori_loop(waited, need, wait_piece, 0)
        for u in range(UNROLL):
            p = step * UNROLL + u
            both = jnp.concatenate([held[plan[0, p]], held[plan[1, p]]], axis=1)
            product = jnp.dot(
                lhs[plan[4, p]],
                jnp.concatenate([both, both], axis=0),
                preferred_element_type=jnp.float32,
            )
            acc[plan[2, p]] += product[:, 0:128]
            acc[plan[3, p]] += product[:, 128:256]
        return need

    waited = lax.fori_loop(0, plan[5, 0], pairs, jnp.int32(0))
    lax.fori_loop(waited, chunks, wait_piece, 0)

    turn = 4 ^ (((z[0] + 1) >> 1) + 1 & 1)

    def move(k, carry):
        near[k] = acc[k]
        near_out[k] = acc[16 + k].astype(jnp.bfloat16)
        away_a[k] = acc[8 + k, 0:128, :]
        away_b[k] = acc[8 + (k ^ turn), 128:256, :]
        away_out[0, k] = acc[24 + k, 0:128, :].astype(jnp.bfloat16)
        away_out[1, k] = acc[24 + (k ^ turn), 128:256, :].astype(jnp.bfloat16)
        return carry

    lax.fori_loop(0, 8, move, 0)


def sparse_product(plan, z, grads, tiles):
    return pl.pallas_call(
        sparse_kernel,
        in_specs=[SMEM, SMEM, VMEM, ANY],
        out_specs=[VMEM] * 5,
        out_shape=[
            jax.ShapeDtypeStruct((8, 256, 128), jnp.float32),
            jax.ShapeDtypeStruct((8, 128, 128), jnp.float32),
            jax.ShapeDtypeStruct((8, 128, 128), jnp.float32),
            jax.ShapeDtypeStruct((8, 256, 128), jnp.bfloat16),
            jax.ShapeDtypeStruct((2, 8, 128, 128), jnp.bfloat16),
        ],
        scratch_shapes=[
            pltpu.VMEM((9, 256, 256), jnp.bfloat16),
            pltpu.VMEM((33, 256, 128), jnp.float32),
            pltpu.VMEM((192, 128, 128), jnp.bfloat16),
            pltpu.SemaphoreType.DMA((192 // CHUNK,)),
        ],
        compiler_params=params(SPARSE_MIB),
        cost_estimate=pl.CostEstimate(flops=4 * 10**9, bytes_accessed=12 * MIB, transcendentals=0),
        name="sparse",
    )(plan, z[None], grads, tiles)


def mid_kernel(away_a, away_b, part, out_a, out_b):
    for k in range(8):
        out_a[k] = (away_a[k] + part[0, k].astype(jnp.float32)).astype(jnp.bfloat16)
        out_b[k] = (away_b[k] + part[1, k].astype(jnp.float32)).astype(jnp.bfloat16)


def mid_part(away_a, away_b, part):
    return pl.pallas_call(
        mid_kernel,
        in_specs=[VMEM] * 3,
        out_specs=[VMEM] * 2,
        out_shape=[jax.ShapeDtypeStruct((8, 128, 128), jnp.bfloat16)] * 2,
        compiler_params=params(8),
        name="mid",
    )(away_a, away_b, part)


def feat_of(low, high, k):
    return (high if k & 2 else low)[(k & 1) * 2 + (k >> 2)]


def base_kernel(near, core_part, feats_low, feats_high, base, total_t):
    total = jnp.zeros((256, 256), jnp.float32)
    for k in range(8):
        block = near[k] + core_part[k].astype(jnp.float32)
        base[k] = block
        high = block.astype(jnp.bfloat16)
        low = (block - high.astype(jnp.float32)).astype(jnp.bfloat16)
        feat = feat_of(feats_low, feats_high, k)
        total += jnp.dot(
            jnp.concatenate([high, low], axis=1),
            jnp.concatenate([feat, feat], axis=0),
            preferred_element_type=jnp.float32,
        )
    total_t[...] = total


def base_part(near, core_part, feats_low, feats_high):
    return pl.pallas_call(
        base_kernel,
        in_specs=[VMEM] * 4,
        out_specs=[VMEM] * 2,
        out_shape=[
            jax.ShapeDtypeStruct((8, 256, 128), jnp.float32),
            jax.ShapeDtypeStruct((256, 256), jnp.float32),
        ],
        compiler_params=params(12),
        cost_estimate=pl.CostEstimate(flops=10**9, bytes_accessed=4 * MIB, transcendentals=0),
        name="base",
    )(near, core_part, feats_low, feats_high)


def neigh_kernel(core, base, part_a, part_b, feats_low, feats_high, total_t, own_self, keep, send, kept, sent):
    total = total_t[...]
    z_part = [jnp.concatenate([part_a[k], part_b[k]], axis=0) for k in range(8)]
    for k in range(0, 8, 2):
        pair = [feat_of(feats_low, feats_high, k + u) for u in range(2)]
        total += jnp.dot(
            jnp.concatenate([z_part[k], z_part[k + 1]], axis=1),
            jnp.concatenate(pair, axis=0),
            preferred_element_type=jnp.float32,
        )
    total = total.T
    for k in range(8):
        block = base[k] + z_part[k].astype(jnp.float32)
        if k < 4:
            keep[k] = block
        else:
            send[k - 4] = block.astype(jnp.bfloat16)
    first = core[0] == 0

    @pl.when(first)
    def _():
        kept[...] = own_self[...]
        sent[...] = total

    @pl.when(jnp.logical_not(first))
    def _():
        kept[...] = total
        sent[...] = own_self[...]


def neigh_part(core, base, part_a, part_b, feats_low, feats_high, total_t, own_self):
    return pl.pallas_call(
        neigh_kernel,
        in_specs=[SMEM] + [VMEM] * 7,
        out_specs=[VMEM] * 4,
        out_shape=[
            jax.ShapeDtypeStruct((4, 256, 128), jnp.float32),
            jax.ShapeDtypeStruct((4, 256, 128), jnp.bfloat16),
            jax.ShapeDtypeStruct((256, 256), jnp.float32),
            jax.ShapeDtypeStruct((256, 256), jnp.float32),
        ],
        compiler_params=params(12),
        cost_estimate=pl.CostEstimate(flops=10**9, bytes_accessed=4 * MIB, transcendentals=0),
        name="neigh",
    )(core[None], base, part_a, part_b, feats_low, feats_high, total_t, own_self)


def fold_kernel(scale, pieces, keep, got, out, *rest):
    total = pieces[0]
    for k in range(1, pieces.shape[0]):
        total += pieces[k]
    total = total * scale
    for k in range(out.shape[0]):
        out[k] = total
    half = keep.shape[0] // 2
    kept, send = rest
    for k in range(half):
        kept[k] = keep[k] + got[k].astype(jnp.float32)
        send[k] = (keep[half + k] + got[half + k].astype(jnp.float32)).astype(jnp.bfloat16)


def fold(scale, pieces, receivers, keep, got):
    half = keep.shape[0] // 2
    return pl.pallas_call(
        functools.partial(fold_kernel, scale),
        in_specs=[VMEM] * 3,
        out_specs=[VMEM] * 3,
        out_shape=[
            jax.ShapeDtypeStruct((receivers, 16, 256), jnp.float32),
            jax.ShapeDtypeStruct((half, 256, 128), jnp.float32),
            jax.ShapeDtypeStruct((half, 256, 128), jnp.bfloat16),
        ],
        compiler_params=params(8),
        name="fold",
    )(pieces, keep, got)


def last_kernel(core, own, part, grads, w_self, w_neigh, full, other, grad_x, grad_self, grad_neigh):
    first = core[0] == 0

    @pl.when(first)
    def _():
        grad_self[...] = full[...]
        grad_neigh[...] = other[...]

    @pl.when(jnp.logical_not(first))
    def _():
        grad_self[...] = other[...]
        grad_neigh[...] = full[...]

    total = own[0] + part[0].astype(jnp.float32)
    high = total.astype(jnp.bfloat16)
    low = (total - high.astype(jnp.float32)).astype(jnp.bfloat16)
    nt = (((1,), (1,)), ((), ()))
    out = lax.dot_general(w_self[...], grads[...], nt, preferred_element_type=jnp.float32)
    out += jnp.dot(w_neigh[...], high, preferred_element_type=jnp.float32)
    out += jnp.dot(w_neigh[...], low, preferred_element_type=jnp.float32)
    grad_x[...] = out.T.astype(jnp.bfloat16)


def last(core, own, part, grads, w_self, w_neigh, full, other):
    return pl.pallas_call(
        last_kernel,
        in_specs=[SMEM] + [VMEM] * 7,
        out_specs=[VMEM] * 3,
        out_shape=[
            jax.ShapeDtypeStruct((128, 256), jnp.bfloat16),
            jax.ShapeDtypeStruct((256, 256), jnp.float32),
            jax.ShapeDtypeStruct((256, 256), jnp.float32),
        ],
        compiler_params=params(8),
        name="last",
    )(core[None], own, part, grads, w_self, w_neigh, full, other)


def swap_z(value, distance):
    return lax.ppermute(value, "row", [(row, row ^ (4 * distance)) for row in range(32)])


def swap_z_other(value):
    pairs = []
    for row in range(32):
        z = row >> 2
        other = (z + 1) % 8 if z & 1 else (z - 1) % 8
        pairs.append((row, other * 4 + (row & 3)))
    return lax.ppermute(value, "row", pairs)


def swap_x(value):
    return lax.ppermute(value, "row", [(row, row ^ 2) for row in range(32)])


def shards(features, grad_out, w_self, w_neigh, tiles, tile_rows, tile_cols, tile_counts, degrees):
    row = lax.axis_index("row").astype(jnp.int32)
    core = row & 1
    node_total = 128 * 256
    group = exchange(head(grad_out, degrees), ("xh", "y"))
    plan, own_self = prep(tile_counts, row, tile_rows, tile_cols, features, grad_out)
    feats = features[None]
    feats = join(feats, swap_z(feats, 2))
    feats_far = swap_z(feats, 4)
    group, feats, plan = lax.optimization_barrier((group, feats, plan))
    near, away_a, away_b, near_out, away_out = sparse_product(plan, row >> 2, group, tiles[0])
    away_out, feats_far = lax.optimization_barrier((away_out, feats_far))
    feats = join(feats, feats_far)
    away_a, away_b = mid_part(away_a, away_b, swap_core(away_out))
    core_part = swap_core(near_out)
    part_a, part_b = swap_z(away_a, 1), swap_z_other(away_b)
    feats_x = swap_x(feats)
    base, total_t = base_part(near, core_part, feats, feats_x)
    keep, send, kept, sent = neigh_part(core, base, part_a, part_b, feats, feats_x, total_t, own_self)
    kept = kept + swap_core(sent)
    got = swap_z(send, 2)
    pieces = exchange(kept.reshape(16, 16, 256), ("xh", "xl", "y"))
    pieces, keep, send = fold(1.0, pieces, 8, keep, got)
    got = swap_x(send)
    pieces = exchange(pieces, ("z",))
    pieces, keep, send = fold(1.0 / node_total, pieces, 16, keep, got)
    got = swap_z(send, 4)
    full = exchange(pieces, ("xh", "xl", "y")).reshape(256, 256)
    full, got = lax.optimization_barrier((full, got))
    other = swap_core(full)
    return last(core, keep, got, grad_out, w_self, w_neigh, full, other)


def solution(mesh):
    in_specs = (
        P(("row", "blk"), None),
        P(("row", "blk"), None),
        P(),
        P(),
        P(("row", "blk"), None, None, None),
        P(("row", "blk"), None),
        P(("row", "blk"), None),
        P(("row", "blk")),
        P(("row", "blk")),
    )
    out_specs = (P(("row", "blk"), None), P(), P())
    return jax.shard_map(shards, mesh=mesh, in_specs=in_specs, out_specs=out_specs, check_vma=False)
```

```python
import functools
import itertools

import jax
import jax.numpy as jnp
from jax import lax
from jax.experimental import pallas as pl
from jax.experimental.pallas import tpu as pltpu
from jax.sharding import PartitionSpec as P

PARTS = {"z": 8, "xl": 2, "core": 2, "xh": 2, "y": 4}
CHUNK = 16
DEG_ROWS = 16
UNROLL = 8
TRASH = 32
ZERO_ROW = 8
MIB = 1024 * 1024
DENSE_FLOPS = 5 * 10**9
SPARSE_MIB = 48
VMEM = pl.BlockSpec(memory_space=pltpu.VMEM)
SMEM = pl.BlockSpec(memory_space=pltpu.SMEM)
ANY = pl.BlockSpec(memory_space=pl.ANY)


def device_id(where):
    row = (where["z"] * 2 + where["xl"]) * 2 + where["core"]
    return row * 8 + where["xh"] * 4 + where["y"]


def groups_of(names):
    rest = [name for name in PARTS if name not in names]
    groups = []
    for fixed in itertools.product(*[range(PARTS[name]) for name in rest]):
        where = dict(zip(rest, fixed))
        group = []
        for moving in itertools.product(*[range(PARTS[name]) for name in names]):
            where.update(zip(names, moving))
            group.append(device_id(where))
        groups.append(group)
    return groups


def exchange(blocks, names):
    return lax.all_to_all(
        blocks, ("row", "blk"), 0, 0, axis_index_groups=groups_of(names), tiled=True
    )


def spread(block, names, count):
    return exchange(jnp.broadcast_to(block[None], (count,) + block.shape), names)


def swap_core(value):
    return lax.ppermute(value, "row", [(row, row ^ 1) for row in range(32)])


def params(mib):
    return pltpu.CompilerParams(vmem_limit_bytes=mib * MIB)


def head_kernel(grads, degrees, out, block, degree, sems):
    loads = [
        pltpu.make_async_copy(degrees, degree, sems.at[8]),
        pltpu.make_async_copy(grads, block.at[pl.ds(0, 128)], sems.at[9]),
    ]
    for load in loads:
        load.start()
    loads[0].wait()
    value = jnp.broadcast_to(degree[...], (DEG_ROWS, 128)).astype(jnp.float32)
    block[128 : 128 + DEG_ROWS, 0:128] = value.astype(jnp.bfloat16)
    block[128 : 128 + DEG_ROWS, 128:256] = jnp.zeros((DEG_ROWS, 128), jnp.bfloat16)
    loads[1].wait()
    stores = [pltpu.make_async_copy(block, out.at[k], sems.at[k]) for k in range(8)]
    for store in stores:
        store.start()
    for store in stores:
        store.wait()


def head(grads, degrees):
    return pl.pallas_call(
        head_kernel,
        in_specs=[ANY, ANY],
        out_specs=ANY,
        out_shape=jax.ShapeDtypeStruct((8, 128 + DEG_ROWS, 256), jnp.bfloat16),
        scratch_shapes=[
            pltpu.VMEM((128 + DEG_ROWS, 256), jnp.bfloat16),
            pltpu.VMEM((1, 128), jnp.int32),
            pltpu.SemaphoreType.DMA((10,)),
        ],
        compiler_params=params(60),
        name="head",
    )(grads, degrees[None])


def prep_kernel(counts, row, *refs):
    sources, (plan, own_self, own), (rows, cols, grads), sems = refs[:4], refs[4:7], refs[7:10], refs[10]
    feats = own.at[0]
    copies = [
        pltpu.make_async_copy(source, target, sems.at[k])
        for k, (source, target) in enumerate(zip(sources, (rows, cols, feats, grads)))
    ]
    for copy in copies:
        copy.start()
    for copy in copies:
        copy.wait()
    own_self[...] = lax.dot_general(
        feats[...], grads[...], (((0,), (0,)), ((), ())), preferred_element_type=jnp.float32
    )
    live = counts[0]
    slots = rows.shape[1]
    slot = lax.broadcasted_iota(jnp.int32, (1, slots), 1)
    lanes = lax.broadcasted_iota(jnp.int32, (8, slots), 0)
    hot = jnp.where((rows[...] == lanes) & (slot < live), 1.0, 0.0)
    earlier = lax.broadcasted_iota(jnp.int32, (slots, slots), 0) < lax.broadcasted_iota(
        jnp.int32, (slots, slots), 1
    )
    earlier = jnp.where(earlier, 1.0, 0.0).astype(jnp.bfloat16)

    def before(flags):
        return jnp.dot(flags.astype(jnp.bfloat16), earlier, preferred_element_type=jnp.float32)

    rank = jnp.sum(hot * before(hot), axis=0, keepdims=True).astype(jnp.int32)
    count = jnp.sum(hot * jnp.sum(hot, axis=1, keepdims=True), axis=0, keepdims=True)
    second = jnp.where((slot < live) & ((rank & 1) == 1), 1.0, 0.0)
    single = jnp.where((slot < live) & ((rank & 1) == 0) & (rank + 1 == count.astype(jnp.int32)), 1.0, 0.0)
    pairs = jnp.sum(second, axis=1, keepdims=True).astype(jnp.int32)
    total = pairs + jnp.sum(single, axis=1, keepdims=True).astype(jnp.int32)
    place_of_second = jnp.where(second > 0, before(jnp.broadcast_to(second, (8, slots)))[0:1], -1.0)
    place_of_single = before(jnp.broadcast_to(single, (8, slots)))[0:1].astype(jnp.int32) + pairs
    place_of_single = jnp.where(single > 0, place_of_single, -1)
    key = jnp.where(slot < live, rows[...] * 256 + (rank >> 1), -1).astype(jnp.float32)
    entry = lax.broadcasted_iota(jnp.int32, (128, slots), 0)
    is_second = jnp.where(entry == place_of_second.astype(jnp.int32), 1.0, 0.0)
    entry_key = jnp.sum(is_second * key, axis=1, keepdims=True)
    is_first = (entry < pairs) & (key == entry_key) & (second == 0)
    is_first = jnp.where(is_first | (entry == place_of_single), 1.0, 0.0)
    far = cols[...] ^ row[0]
    place = (far & 1) * 16 + (far & 4) * 2 + (far & 8) // 2 + (far & 2) + (far >> 4)
    values = jnp.where(lanes == 0, slot, 0) + jnp.where(lanes == 1, place, 0)
    values += jnp.where(lanes == 2, rows[...], 0) + jnp.where(lanes == 3, 1, 0)
    values = values.astype(jnp.float32).astype(jnp.bfloat16)

    def pick(chosen):
        nt = (((1,), (1,)), ((), ()))
        chosen = chosen.astype(jnp.bfloat16)
        return lax.dot_general(values, chosen, nt, preferred_element_type=jnp.float32).astype(jnp.int32)

    one, two = pick(is_first), pick(is_second)
    plan[0:1, :] = one[0:1]
    plan[1:2, :] = two[0:1]
    plan[2:3, :] = one[1:2] + (1 - one[3:4]) * TRASH
    plan[3:4, :] = two[1:2] + (1 - two[3:4]) * TRASH
    plan[4:5, :] = one[2:3] + (1 - one[3:4]) * ZERO_ROW
    plan[5:6, :] = jnp.broadcast_to((total + UNROLL - 1) >> 3, (1, 128))
    plan[6:7, :] = (jnp.maximum(one[0:1], two[0:1]) >> 4) + 1
    plan[7:8, :] = jnp.full((1, 128), (live + CHUNK - 1) >> 4, jnp.int32)


def prep(counts, row, rows, cols, feats, grads):
    return pl.pallas_call(
        prep_kernel,
        in_specs=[SMEM, SMEM, ANY, ANY, ANY, ANY],
        out_specs=[VMEM, VMEM, VMEM],
        out_shape=[
            jax.ShapeDtypeStruct((8, 128), jnp.int32),
            jax.ShapeDtypeStruct((256, 256), jnp.float32),
            jax.ShapeDtypeStruct((1, 128, 256), jnp.bfloat16),
        ],
        scratch_shapes=[
            pltpu.VMEM(rows.shape, jnp.int32),
            pltpu.VMEM(cols.shape, jnp.int32),
            pltpu.VMEM(grads.shape, jnp.bfloat16),
            pltpu.SemaphoreType.DMA((4,)),
        ],
        compiler_params=params(60),
        cost_estimate=pl.CostEstimate(flops=0, bytes_accessed=4 * MIB, transcendentals=0),
        name="prep",
    )(counts, row[None], rows, cols, feats, grads)


def join_kernel(*refs):
    for k, ref in enumerate(refs[:-1]):
        refs[-1][k] = ref[0]


def join(*blocks):
    return pl.pallas_call(
        join_kernel,
        in_specs=[VMEM] * len(blocks),
        out_specs=VMEM,
        out_shape=jax.ShapeDtypeStruct((len(blocks),) + blocks[0].shape[1:], blocks[0].dtype),
        compiler_params=params(4),
        name="join",
    )(*blocks)


def sparse_kernel(plan, z, grads, tiles, near, away_a, away_b, near_out, away_out, lhs, acc, held, sems):
    chunks = plan[7, 0]

    def piece(k):
        part = pl.ds(k * CHUNK, CHUNK)
        return pltpu.make_async_copy(tiles.at[part], held.at[part], sems.at[k])

    def wait_piece(k, carry):
        piece(k).wait()
        return carry

    for k in range(192 // CHUNK):
        pl.when(k < chunks)(lambda k=k: piece(k).start())
    for k in range(8):
        grad_t = grads[k, 0:128, :].T.astype(jnp.float32)
        degree = 1.0 / grads[k, 128:129, 0:128].astype(jnp.float32)
        value = grad_t * degree
        high = value.astype(jnp.bfloat16)
        low = (value - high.astype(jnp.float32)).astype(jnp.bfloat16)
        lhs[k, :, 0:128] = high
        lhs[k, :, 128:256] = low
    lhs[ZERO_ROW] = jnp.zeros((256, 256), jnp.bfloat16)

    def clear(k, carry):
        acc[k] = jnp.zeros((256, 128), jnp.float32)
        return carry

    lax.fori_loop(0, 33, clear, 0)

    def pairs(step, waited):
        need = waited
        for u in range(UNROLL):
            need = jnp.maximum(need, plan[6, step * UNROLL + u])
        lax.fori_loop(waited, need, wait_piece, 0)
        for u in range(UNROLL):
            p = step * UNROLL + u
            both = jnp.concatenate([held[plan[0, p]], held[plan[1, p]]], axis=1)
            product = jnp.dot(
                lhs[plan[4, p]],
                jnp.concatenate([both, both], axis=0),
                preferred_element_type=jnp.float32,
            )
            acc[plan[2, p]] += product[:, 0:128]
            acc[plan[3, p]] += product[:, 128:256]
        return need

    waited = lax.fori_loop(0, plan[5, 0], pairs, jnp.int32(0))
    lax.fori_loop(waited, chunks, wait_piece, 0)

    turn = 4 ^ (((z[0] + 1) >> 1) + 1 & 1)

    def move(k, carry):
        near[k] = acc[k]
        near_out[k] = acc[16 + k].astype(jnp.bfloat16)
        away_a[k] = acc[8 + k, 0:128, :]
        away_b[k] = acc[8 + (k ^ turn), 128:256, :]
        away_out[0, k] = acc[24 + k, 0:128, :].astype(jnp.bfloat16)
        away_out[1, k] = acc[24 + (k ^ turn), 128:256, :].astype(jnp.bfloat16)
        return carry

    lax.fori_loop(0, 8, move, 0)


def sparse_product(plan, z, grads, tiles):
    return pl.pallas_call(
        sparse_kernel,
        in_specs=[SMEM, SMEM, VMEM, ANY],
        out_specs=[VMEM] * 5,
        out_shape=[
            jax.ShapeDtypeStruct((8, 256, 128), jnp.float32),
            jax.ShapeDtypeStruct((8, 128, 128), jnp.float32),
            jax.ShapeDtypeStruct((8, 128, 128), jnp.float32),
            jax.ShapeDtypeStruct((8, 256, 128), jnp.bfloat16),
            jax.ShapeDtypeStruct((2, 8, 128, 128), jnp.bfloat16),
        ],
        scratch_shapes=[
            pltpu.VMEM((9, 256, 256), jnp.bfloat16),
            pltpu.VMEM((33, 256, 128), jnp.float32),
            pltpu.VMEM((192, 128, 128), jnp.bfloat16),
            pltpu.SemaphoreType.DMA((192 // CHUNK,)),
        ],
        compiler_params=params(SPARSE_MIB),
        cost_estimate=pl.CostEstimate(flops=4 * 10**9, bytes_accessed=12 * MIB, transcendentals=0),
        name="sparse",
    )(plan, z[None], grads, tiles)


def mid_kernel(away_a, away_b, part, out_a, out_b):
    for k in range(8):
        out_a[k] = (away_a[k] + part[0, k].astype(jnp.float32)).astype(jnp.bfloat16)
        out_b[k] = (away_b[k] + part[1, k].astype(jnp.float32)).astype(jnp.bfloat16)


def mid_part(away_a, away_b, part):
    return pl.pallas_call(
        mid_kernel,
        in_specs=[VMEM] * 3,
        out_specs=[VMEM] * 2,
        out_shape=[jax.ShapeDtypeStruct((8, 128, 128), jnp.bfloat16)] * 2,
        compiler_params=params(8),
        name="mid",
    )(away_a, away_b, part)


def feat_of(z, low, high, k):
    turn = z[0] & 2
    place = [0, 1 + turn, 2, 3 - turn][(k & 1) * 2 + (k >> 2)]
    return (high if k & 2 else low)[place]


def base_kernel(z, near, core_part, feats_low, feats_high, base, total_t):
    total = jnp.zeros((256, 256), jnp.float32)
    for k in range(8):
        block = near[k] + core_part[k].astype(jnp.float32)
        base[k] = block
        high = block.astype(jnp.bfloat16)
        low = (block - high.astype(jnp.float32)).astype(jnp.bfloat16)
        feat = feat_of(z, feats_low, feats_high, k)
        total += jnp.dot(
            jnp.concatenate([high, low], axis=1),
            jnp.concatenate([feat, feat], axis=0),
            preferred_element_type=jnp.float32,
        )
    total_t[...] = total


def base_part(z, near, core_part, feats_low, feats_high):
    return pl.pallas_call(
        base_kernel,
        in_specs=[SMEM] + [VMEM] * 4,
        out_specs=[VMEM] * 2,
        out_shape=[
            jax.ShapeDtypeStruct((8, 256, 128), jnp.float32),
            jax.ShapeDtypeStruct((256, 256), jnp.float32),
        ],
        compiler_params=params(12),
        cost_estimate=pl.CostEstimate(flops=10**9, bytes_accessed=4 * MIB, transcendentals=0),
        name="base",
    )(z[None], near, core_part, feats_low, feats_high)


def neigh_kernel(core, z, base, part_a, part_b, feats_low, feats_high, total_t, own_self, keep, send, kept, sent):
    total = total_t[...]
    z_part = [jnp.concatenate([part_a[k], part_b[k]], axis=0) for k in range(8)]
    for k in range(0, 8, 2):
        pair = [feat_of(z, feats_low, feats_high, k + u) for u in range(2)]
        total += jnp.dot(
            jnp.concatenate([z_part[k], z_part[k + 1]], axis=1),
            jnp.concatenate(pair, axis=0),
            preferred_element_type=jnp.float32,
        )
    total = total.T
    for k in range(8):
        block = base[k] + z_part[k].astype(jnp.float32)
        if k < 4:
            keep[k] = block
        else:
            send[k - 4] = block.astype(jnp.bfloat16)
    first = core[0] == 0

    @pl.when(first)
    def _():
        kept[...] = own_self[...]
        sent[...] = total

    @pl.when(jnp.logical_not(first))
    def _():
        kept[...] = total
        sent[...] = own_self[...]


def neigh_part(core, z, base, part_a, part_b, feats_low, feats_high, total_t, own_self):
    return pl.pallas_call(
        neigh_kernel,
        in_specs=[SMEM] * 2 + [VMEM] * 7,
        out_specs=[VMEM] * 4,
        out_shape=[
            jax.ShapeDtypeStruct((4, 256, 128), jnp.float32),
            jax.ShapeDtypeStruct((4, 256, 128), jnp.bfloat16),
            jax.ShapeDtypeStruct((256, 256), jnp.float32),
            jax.ShapeDtypeStruct((256, 256), jnp.float32),
        ],
        compiler_params=params(12),
        cost_estimate=pl.CostEstimate(flops=10**9, bytes_accessed=4 * MIB, transcendentals=0),
        name="neigh",
    )(core[None], z[None], base, part_a, part_b, feats_low, feats_high, total_t, own_self)


def fold_kernel(scale, pieces, keep, got, out, *rest):
    total = pieces[0]
    for k in range(1, pieces.shape[0]):
        total += pieces[k]
    total = total * scale
    for k in range(out.shape[0]):
        out[k] = total
    half = keep.shape[0] // 2
    kept, send = rest
    for k in range(half):
        kept[k] = keep[k] + got[k].astype(jnp.float32)
        send[k] = (keep[half + k] + got[half + k].astype(jnp.float32)).astype(jnp.bfloat16)


def fold(scale, pieces, receivers, keep, got):
    half = keep.shape[0] // 2
    return pl.pallas_call(
        functools.partial(fold_kernel, scale),
        in_specs=[VMEM] * 3,
        out_specs=[VMEM] * 3,
        out_shape=[
            jax.ShapeDtypeStruct((receivers, 16, 256), jnp.float32),
            jax.ShapeDtypeStruct((half, 256, 128), jnp.float32),
            jax.ShapeDtypeStruct((half, 256, 128), jnp.bfloat16),
        ],
        compiler_params=params(8),
        name="fold",
    )(pieces, keep, got)


def dense_kernel(own, part, grads, w_self, w_neigh, grad_x):
    total = own[0] + part[0].astype(jnp.float32)
    high = total.astype(jnp.bfloat16)
    low = (total - high.astype(jnp.float32)).astype(jnp.bfloat16)
    nt = (((1,), (1,)), ((), ()))
    out = lax.dot_general(w_self[...], grads[...], nt, preferred_element_type=jnp.float32)
    out += jnp.dot(w_neigh[...], high, preferred_element_type=jnp.float32)
    out += jnp.dot(w_neigh[...], low, preferred_element_type=jnp.float32)
    grad_x[...] = out.T.astype(jnp.bfloat16)


def dense(own, part, grads, w_self, w_neigh):
    return pl.pallas_call(
        dense_kernel,
        in_specs=[VMEM] * 5,
        out_specs=VMEM,
        out_shape=jax.ShapeDtypeStruct((128, 256), jnp.bfloat16),
        compiler_params=params(8),
        cost_estimate=pl.CostEstimate(flops=DENSE_FLOPS, bytes_accessed=MIB, transcendentals=0),
        name="dense",
    )(own, part, grads, w_self, w_neigh)


def last_kernel(core, full, other, grad_self, grad_neigh):
    first = core[0] == 0

    @pl.when(first)
    def _():
        grad_self[...] = full[...]
        grad_neigh[...] = other[...]

    @pl.when(jnp.logical_not(first))
    def _():
        grad_self[...] = other[...]
        grad_neigh[...] = full[...]


def last(core, full, other):
    return pl.pallas_call(
        last_kernel,
        in_specs=[SMEM] + [VMEM] * 2,
        out_specs=[VMEM] * 2,
        out_shape=[jax.ShapeDtypeStruct((256, 256), jnp.float32)] * 2,
        compiler_params=params(8),
        name="last",
    )(core[None], full, other)


def swap_z(value, distance):
    return lax.ppermute(value, "row", [(row, row ^ (4 * distance)) for row in range(32)])


def shift_z(value, steps):
    pairs = [(row, (row + 4 * steps) % 32) for row in range(32)]
    return lax.ppermute(value, "row", pairs)


def swap_z_other(value):
    pairs = []
    for row in range(32):
        z = row >> 2
        other = (z + 1) % 8 if z & 1 else (z - 1) % 8
        pairs.append((row, other * 4 + (row & 3)))
    return lax.ppermute(value, "row", pairs)


def swap_x(value):
    return lax.ppermute(value, "row", [(row, row ^ 2) for row in range(32)])


def shards(features, grad_out, w_self, w_neigh, tiles, tile_rows, tile_cols, tile_counts, degrees):
    row = lax.axis_index("row").astype(jnp.int32)
    core = row & 1
    node_total = 128 * 256
    group = exchange(head(grad_out, degrees), ("xh", "y"))
    plan, own_self, own = prep(tile_counts, row, tile_rows, tile_cols, features, grad_out)
    z = row >> 2
    above, below = shift_z(features[None], 6), shift_z(features[None], 2)
    opposite = shift_z(above, 6)
    group, above, below, plan = lax.optimization_barrier((group, above, below, plan))
    near, away_a, away_b, near_out, away_out = sparse_product(plan, z, group, tiles[0])
    away_out, opposite = lax.optimization_barrier((away_out, opposite))
    feats = join(own, above, opposite, below)
    away_a, away_b = mid_part(away_a, away_b, swap_core(away_out))
    core_part = swap_core(near_out)
    part_a, part_b = swap_z(away_a, 1), swap_z_other(away_b)
    feats_x = swap_x(feats)
    base, total_t = base_part(z, near, core_part, feats, feats_x)
    keep, send, kept, sent = neigh_part(core, z, base, part_a, part_b, feats, feats_x, total_t, own_self)
    kept = kept + swap_core(sent)
    got = swap_z(send, 2)
    pieces = exchange(kept.reshape(16, 16, 256), ("xh", "xl", "y"))
    pieces, keep, send = fold(1.0, pieces, 8, keep, got)
    got = swap_x(send)
    pieces = exchange(pieces, ("z",))
    pieces, keep, send = fold(1.0 / node_total, pieces, 16, keep, got)
    got = swap_z(send, 4)
    full = exchange(pieces, ("xh", "xl", "y")).reshape(256, 256)
    other = swap_core(full)
    grad_x = dense(keep, got, grad_out, w_self, w_neigh)
    grad_self, grad_neigh = last(core, full, other)
    return grad_x, grad_self, grad_neigh


def solution(mesh):
    in_specs = (
        P(("row", "blk"), None),
        P(("row", "blk"), None),
        P(),
        P(),
        P(("row", "blk"), None, None, None),
        P(("row", "blk"), None),
        P(("row", "blk"), None),
        P(("row", "blk")),
        P(("row", "blk")),
    )
    out_specs = (P(("row", "blk"), None), P(), P())
    return jax.shard_map(shards, mesh=mesh, in_specs=in_specs, out_specs=out_specs, check_vma=False)
```

```python
import functools
import itertools

import jax
import jax.numpy as jnp
from jax import lax
from jax.experimental import pallas as pl
from jax.experimental.pallas import tpu as pltpu
from jax.sharding import PartitionSpec as P

PARTS = {"z": 8, "xl": 2, "core": 2, "xh": 2, "y": 4}
CHUNK = 16
DEG_ROWS = 16
UNROLL = 8
TRASH = 32
ZERO_ROW = 8
MIB = 1024 * 1024
DENSE_FLOPS = 5 * 10**9
SPARSE_MIB = 48
VMEM = pl.BlockSpec(memory_space=pltpu.VMEM)
SMEM = pl.BlockSpec(memory_space=pltpu.SMEM)
ANY = pl.BlockSpec(memory_space=pl.ANY)


def device_id(where):
    row = (where["z"] * 2 + where["xl"]) * 2 + where["core"]
    return row * 8 + where["xh"] * 4 + where["y"]


def groups_of(names):
    rest = [name for name in PARTS if name not in names]
    groups = []
    for fixed in itertools.product(*[range(PARTS[name]) for name in rest]):
        where = dict(zip(rest, fixed))
        group = []
        for moving in itertools.product(*[range(PARTS[name]) for name in names]):
            where.update(zip(names, moving))
            group.append(device_id(where))
        groups.append(group)
    return groups


def exchange(blocks, names):
    return lax.all_to_all(
        blocks, ("row", "blk"), 0, 0, axis_index_groups=groups_of(names), tiled=True
    )


def spread(block, names, count):
    return exchange(jnp.broadcast_to(block[None], (count,) + block.shape), names)


def swap_core(value):
    return lax.ppermute(value, "row", [(row, row ^ 1) for row in range(32)])


def params(mib):
    return pltpu.CompilerParams(vmem_limit_bytes=mib * MIB)


def head_kernel(grads, degrees, out, block, degree, sems):
    loads = [
        pltpu.make_async_copy(degrees, degree, sems.at[8]),
        pltpu.make_async_copy(grads, block.at[pl.ds(0, 128)], sems.at[9]),
    ]
    for load in loads:
        load.start()
    loads[0].wait()
    value = jnp.broadcast_to(degree[...], (DEG_ROWS, 128)).astype(jnp.float32)
    block[128 : 128 + DEG_ROWS, 0:128] = value.astype(jnp.bfloat16)
    block[128 : 128 + DEG_ROWS, 128:256] = jnp.zeros((DEG_ROWS, 128), jnp.bfloat16)
    loads[1].wait()
    stores = [pltpu.make_async_copy(block, out.at[k], sems.at[k]) for k in range(8)]
    for store in stores:
        store.start()
    for store in stores:
        store.wait()


def head(grads, degrees):
    return pl.pallas_call(
        head_kernel,
        in_specs=[ANY, ANY],
        out_specs=ANY,
        out_shape=jax.ShapeDtypeStruct((8, 128 + DEG_ROWS, 256), jnp.bfloat16),
        scratch_shapes=[
            pltpu.VMEM((128 + DEG_ROWS, 256), jnp.bfloat16),
            pltpu.VMEM((1, 128), jnp.int32),
            pltpu.SemaphoreType.DMA((10,)),
        ],
        compiler_params=params(60),
        name="head",
    )(grads, degrees[None])


def self_kernel(feats, grads, own_self):
    own_self[...] = lax.dot_general(
        feats[0], grads[...], (((0,), (0,)), ((), ())), preferred_element_type=jnp.float32
    )


def self_part(feats, grads):
    return pl.pallas_call(
        self_kernel,
        in_specs=[VMEM, VMEM],
        out_specs=VMEM,
        out_shape=jax.ShapeDtypeStruct((256, 256), jnp.float32),
        compiler_params=params(4),
        name="self",
    )(feats, grads)


def prep_kernel(counts, row, rows, cols, feats, plan, own):
    own[0] = feats[...]
    live = counts[0]
    slots = rows.shape[1]
    slot = lax.broadcasted_iota(jnp.int32, (1, slots), 1)
    lanes = lax.broadcasted_iota(jnp.int32, (8, slots), 0)
    hot = jnp.where((rows[...] == lanes) & (slot < live), 1.0, 0.0)
    earlier = lax.broadcasted_iota(jnp.int32, (slots, slots), 0) < lax.broadcasted_iota(
        jnp.int32, (slots, slots), 1
    )
    earlier = jnp.where(earlier, 1.0, 0.0).astype(jnp.bfloat16)

    def before(flags):
        return jnp.dot(flags.astype(jnp.bfloat16), earlier, preferred_element_type=jnp.float32)

    rank = jnp.sum(hot * before(hot), axis=0, keepdims=True).astype(jnp.int32)
    count = jnp.sum(hot * jnp.sum(hot, axis=1, keepdims=True), axis=0, keepdims=True)
    second = jnp.where((slot < live) & ((rank & 1) == 1), 1.0, 0.0)
    single = jnp.where((slot < live) & ((rank & 1) == 0) & (rank + 1 == count.astype(jnp.int32)), 1.0, 0.0)
    pairs = jnp.sum(second, axis=1, keepdims=True).astype(jnp.int32)
    total = pairs + jnp.sum(single, axis=1, keepdims=True).astype(jnp.int32)
    place_of_second = jnp.where(second > 0, before(jnp.broadcast_to(second, (8, slots)))[0:1], -1.0)
    place_of_single = before(jnp.broadcast_to(single, (8, slots)))[0:1].astype(jnp.int32) + pairs
    place_of_single = jnp.where(single > 0, place_of_single, -1)
    key = jnp.where(slot < live, rows[...] * 256 + (rank >> 1), -1).astype(jnp.float32)
    entry = lax.broadcasted_iota(jnp.int32, (128, slots), 0)
    is_second = jnp.where(entry == place_of_second.astype(jnp.int32), 1.0, 0.0)
    entry_key = jnp.sum(is_second * key, axis=1, keepdims=True)
    is_first = (entry < pairs) & (key == entry_key) & (second == 0)
    is_first = jnp.where(is_first | (entry == place_of_single), 1.0, 0.0)
    far = cols[...] ^ row[0]
    place = (far & 1) * 16 + (far & 4) * 2 + (far & 8) // 2 + (far & 2) + (far >> 4)
    values = jnp.where(lanes == 0, slot, 0) + jnp.where(lanes == 1, place, 0)
    values += jnp.where(lanes == 2, rows[...], 0) + jnp.where(lanes == 3, 1, 0)
    values = values.astype(jnp.float32).astype(jnp.bfloat16)

    def pick(chosen):
        nt = (((1,), (1,)), ((), ()))
        chosen = chosen.astype(jnp.bfloat16)
        return lax.dot_general(values, chosen, nt, preferred_element_type=jnp.float32).astype(jnp.int32)

    one, two = pick(is_first), pick(is_second)
    plan[0:1, :] = one[0:1]
    plan[1:2, :] = two[0:1]
    plan[2:3, :] = one[1:2] + (1 - one[3:4]) * TRASH
    plan[3:4, :] = two[1:2] + (1 - two[3:4]) * TRASH
    plan[4:5, :] = one[2:3] + (1 - one[3:4]) * ZERO_ROW
    plan[5:6, :] = jnp.broadcast_to((total + UNROLL - 1) >> 3, (1, 128))
    plan[6:7, :] = (jnp.maximum(one[0:1], two[0:1]) >> 4) + 1
    plan[7:8, :] = jnp.full((1, 128), (live + CHUNK - 1) >> 4, jnp.int32)


def prep(counts, row, rows, cols, feats):
    return pl.pallas_call(
        prep_kernel,
        in_specs=[SMEM, SMEM, VMEM, VMEM, VMEM],
        out_specs=[VMEM, VMEM],
        out_shape=[
            jax.ShapeDtypeStruct((8, 128), jnp.int32),
            jax.ShapeDtypeStruct((1, 128, 256), jnp.bfloat16),
        ],
        compiler_params=params(10),
        cost_estimate=pl.CostEstimate(flops=0, bytes_accessed=4 * MIB, transcendentals=0),
        name="prep",
    )(counts, row[None], rows, cols, feats)


def join_kernel(*refs):
    for k, ref in enumerate(refs[:-1]):
        refs[-1][k] = ref[0]


def join(*blocks):
    return pl.pallas_call(
        join_kernel,
        in_specs=[VMEM] * len(blocks),
        out_specs=VMEM,
        out_shape=jax.ShapeDtypeStruct((len(blocks),) + blocks[0].shape[1:], blocks[0].dtype),
        compiler_params=params(4),
        name="join",
    )(*blocks)


def sparse_kernel(plan, z, grads, tiles, near, away_a, away_b, near_out, away_out, lhs, acc, held, sems):
    chunks = plan[7, 0]

    def piece(k):
        part = pl.ds(k * CHUNK, CHUNK)
        return pltpu.make_async_copy(tiles.at[part], held.at[part], sems.at[k])

    def wait_piece(k, carry):
        piece(k).wait()
        return carry

    for k in range(192 // CHUNK):
        pl.when(k < chunks)(lambda k=k: piece(k).start())
    for k in range(8):
        grad_t = grads[k, 0:128, :].T.astype(jnp.float32)
        degree = 1.0 / grads[k, 128:129, 0:128].astype(jnp.float32)
        value = grad_t * degree
        high = value.astype(jnp.bfloat16)
        low = (value - high.astype(jnp.float32)).astype(jnp.bfloat16)
        lhs[k, :, 0:128] = high
        lhs[k, :, 128:256] = low
    lhs[ZERO_ROW] = jnp.zeros((256, 256), jnp.bfloat16)

    for k in range(32):
        acc[k] = jnp.zeros((256, 128), jnp.float32)

    def pairs(step, waited):
        need = waited
        for u in range(UNROLL):
            need = jnp.maximum(need, plan[6, step * UNROLL + u])
        lax.fori_loop(waited, need, wait_piece, 0)
        for u in range(UNROLL):
            p = step * UNROLL + u
            both = jnp.concatenate([held[plan[0, p]], held[plan[1, p]]], axis=1)
            product = jnp.dot(
                lhs[plan[4, p]],
                jnp.concatenate([both, both], axis=0),
                preferred_element_type=jnp.float32,
            )
            acc[plan[2, p]] += product[:, 0:128]
            acc[plan[3, p]] += product[:, 128:256]
        return need

    waited = lax.fori_loop(0, plan[5, 0], pairs, jnp.int32(0))
    lax.fori_loop(waited, chunks, wait_piece, 0)

    turn = 4 ^ (((z[0] + 1) >> 1) + 1 & 1)

    def move(k, carry):
        near[k] = acc[k]
        near_out[k] = acc[16 + k].astype(jnp.bfloat16)
        away_a[k] = acc[8 + k, 0:128, :]
        away_b[k] = acc[8 + (k ^ turn), 128:256, :]
        away_out[0, k] = acc[24 + k, 0:128, :].astype(jnp.bfloat16)
        away_out[1, k] = acc[24 + (k ^ turn), 128:256, :].astype(jnp.bfloat16)
        return carry

    lax.fori_loop(0, 8, move, 0)


def sparse_product(plan, z, grads, tiles):
    return pl.pallas_call(
        sparse_kernel,
        in_specs=[SMEM, SMEM, VMEM, ANY],
        out_specs=[VMEM] * 5,
        out_shape=[
            jax.ShapeDtypeStruct((8, 256, 128), jnp.float32),
            jax.ShapeDtypeStruct((8, 128, 128), jnp.float32),
            jax.ShapeDtypeStruct((8, 128, 128), jnp.float32),
            jax.ShapeDtypeStruct((8, 256, 128), jnp.bfloat16),
            jax.ShapeDtypeStruct((2, 8, 128, 128), jnp.bfloat16),
        ],
        scratch_shapes=[
            pltpu.VMEM((9, 256, 256), jnp.bfloat16),
            pltpu.VMEM((33, 256, 128), jnp.float32),
            pltpu.VMEM((192, 128, 128), jnp.bfloat16),
            pltpu.SemaphoreType.DMA((192 // CHUNK,)),
        ],
        compiler_params=params(SPARSE_MIB),
        cost_estimate=pl.CostEstimate(flops=4 * 10**9, bytes_accessed=12 * MIB, transcendentals=0),
        name="sparse",
    )(plan, z[None], grads, tiles)


def mid_kernel(away_a, away_b, part, out_a, out_b):
    for k in range(8):
        out_a[k] = (away_a[k] + part[0, k].astype(jnp.float32)).astype(jnp.bfloat16)
        out_b[k] = (away_b[k] + part[1, k].astype(jnp.float32)).astype(jnp.bfloat16)


def mid_part(away_a, away_b, part):
    return pl.pallas_call(
        mid_kernel,
        in_specs=[VMEM] * 3,
        out_specs=[VMEM] * 2,
        out_shape=[jax.ShapeDtypeStruct((8, 128, 128), jnp.bfloat16)] * 2,
        compiler_params=params(8),
        name="mid",
    )(away_a, away_b, part)


def feat_of(z, low, high, k):
    turn = z[0] & 2
    place = [0, 1 + turn, 2, 3 - turn][(k & 1) * 2 + (k >> 2)]
    return (high if k & 2 else low)[place]


def base_kernel(z, near, core_part, feats_low, feats_high, base, total_t):
    total = jnp.zeros((256, 256), jnp.float32)
    for k in range(8):
        block = near[k] + core_part[k].astype(jnp.float32)
        base[k] = block
        high = block.astype(jnp.bfloat16)
        low = (block - high.astype(jnp.float32)).astype(jnp.bfloat16)
        feat = feat_of(z, feats_low, feats_high, k)
        total += jnp.dot(
            jnp.concatenate([high, low], axis=1),
            jnp.concatenate([feat, feat], axis=0),
            preferred_element_type=jnp.float32,
        )
    total_t[...] = total


def base_part(z, near, core_part, feats_low, feats_high):
    return pl.pallas_call(
        base_kernel,
        in_specs=[SMEM] + [VMEM] * 4,
        out_specs=[VMEM] * 2,
        out_shape=[
            jax.ShapeDtypeStruct((8, 256, 128), jnp.float32),
            jax.ShapeDtypeStruct((256, 256), jnp.float32),
        ],
        compiler_params=params(12),
        cost_estimate=pl.CostEstimate(flops=10**9, bytes_accessed=4 * MIB, transcendentals=0),
        name="base",
    )(z[None], near, core_part, feats_low, feats_high)


def neigh_kernel(core, z, base, part_a, part_b, feats_low, feats_high, total_t, own_self, keep, send, kept, sent):
    total = total_t[...]
    z_part = [jnp.concatenate([part_a[k], part_b[k]], axis=0) for k in range(8)]
    for k in range(0, 8, 2):
        pair = [feat_of(z, feats_low, feats_high, k + u) for u in range(2)]
        total += jnp.dot(
            jnp.concatenate([z_part[k], z_part[k + 1]], axis=1),
            jnp.concatenate(pair, axis=0),
            preferred_element_type=jnp.float32,
        )
    total = total.T
    for k in range(8):
        block = base[k] + z_part[k].astype(jnp.float32)
        if k < 4:
            keep[k] = block
        else:
            send[k - 4] = block.astype(jnp.bfloat16)
    first = core[0] == 0

    @pl.when(first)
    def _():
        kept[...] = own_self[...]
        sent[...] = total

    @pl.when(jnp.logical_not(first))
    def _():
        kept[...] = total
        sent[...] = own_self[...]


def neigh_part(core, z, base, part_a, part_b, feats_low, feats_high, total_t, own_self):
    return pl.pallas_call(
        neigh_kernel,
        in_specs=[SMEM] * 2 + [VMEM] * 7,
        out_specs=[VMEM] * 4,
        out_shape=[
            jax.ShapeDtypeStruct((4, 256, 128), jnp.float32),
            jax.ShapeDtypeStruct((4, 256, 128), jnp.bfloat16),
            jax.ShapeDtypeStruct((256, 256), jnp.float32),
            jax.ShapeDtypeStruct((256, 256), jnp.float32),
        ],
        compiler_params=params(12),
        cost_estimate=pl.CostEstimate(flops=10**9, bytes_accessed=4 * MIB, transcendentals=0),
        name="neigh",
    )(core[None], z[None], base, part_a, part_b, feats_low, feats_high, total_t, own_self)


def fold_kernel(scale, pieces, keep, got, out, *rest):
    total = pieces[0]
    for k in range(1, pieces.shape[0]):
        total += pieces[k]
    total = total * scale
    for k in range(out.shape[0]):
        out[k] = total
    half = keep.shape[0] // 2
    kept, send = rest
    for k in range(half):
        kept[k] = keep[k] + got[k].astype(jnp.float32)
        send[k] = (keep[half + k] + got[half + k].astype(jnp.float32)).astype(jnp.bfloat16)


def fold(scale, pieces, receivers, keep, got):
    half = keep.shape[0] // 2
    return pl.pallas_call(
        functools.partial(fold_kernel, scale),
        in_specs=[VMEM] * 3,
        out_specs=[VMEM] * 3,
        out_shape=[
            jax.ShapeDtypeStruct((receivers, 16, 256), jnp.float32),
            jax.ShapeDtypeStruct((half, 256, 128), jnp.float32),
            jax.ShapeDtypeStruct((half, 256, 128), jnp.bfloat16),
        ],
        compiler_params=params(8),
        name="fold",
    )(pieces, keep, got)


def dense_kernel(own, part, grads, w_self, w_neigh, grad_x):
    total = own[0] + part[0].astype(jnp.float32)
    high = total.astype(jnp.bfloat16)
    low = (total - high.astype(jnp.float32)).astype(jnp.bfloat16)
    nt = (((1,), (1,)), ((), ()))
    out = lax.dot_general(w_self[...], grads[...], nt, preferred_element_type=jnp.float32)
    out += jnp.dot(w_neigh[...], high, preferred_element_type=jnp.float32)
    out += jnp.dot(w_neigh[...], low, preferred_element_type=jnp.float32)
    grad_x[...] = out.T.astype(jnp.bfloat16)


def dense(own, part, grads, w_self, w_neigh):
    return pl.pallas_call(
        dense_kernel,
        in_specs=[VMEM] * 5,
        out_specs=VMEM,
        out_shape=jax.ShapeDtypeStruct((128, 256), jnp.bfloat16),
        compiler_params=params(8),
        cost_estimate=pl.CostEstimate(flops=DENSE_FLOPS, bytes_accessed=MIB, transcendentals=0),
        name="dense",
    )(own, part, grads, w_self, w_neigh)


def last_kernel(core, full, other, done_x, grad_self, grad_neigh, grad_x):
    first = core[0] == 0
    grad_x[...] = done_x[...]

    @pl.when(first)
    def _():
        grad_self[...] = full[...]
        grad_neigh[...] = other[...]

    @pl.when(jnp.logical_not(first))
    def _():
        grad_self[...] = other[...]
        grad_neigh[...] = full[...]


def last(core, full, other, done_x):
    return pl.pallas_call(
        last_kernel,
        in_specs=[SMEM] + [VMEM] * 3,
        out_specs=[VMEM] * 3,
        out_shape=[
            jax.ShapeDtypeStruct((256, 256), jnp.float32),
            jax.ShapeDtypeStruct((256, 256), jnp.float32),
            jax.ShapeDtypeStruct((128, 256), jnp.bfloat16),
        ],
        compiler_params=params(8),
        name="last",
    )(core[None], full, other, done_x)


def swap_z(value, distance):
    return lax.ppermute(value, "row", [(row, row ^ (4 * distance)) for row in range(32)])


def shift_z(value, steps):
    pairs = [(row, (row + 4 * steps) % 32) for row in range(32)]
    return lax.ppermute(value, "row", pairs)


def swap_z_other(value):
    pairs = []
    for row in range(32):
        z = row >> 2
        other = (z + 1) % 8 if z & 1 else (z - 1) % 8
        pairs.append((row, other * 4 + (row & 3)))
    return lax.ppermute(value, "row", pairs)


def swap_x(value):
    return lax.ppermute(value, "row", [(row, row ^ 2) for row in range(32)])


def shards(features, grad_out, w_self, w_neigh, tiles, tile_rows, tile_cols, tile_counts, degrees):
    row = lax.axis_index("row").astype(jnp.int32)
    core = row & 1
    node_total = 128 * 256
    group = exchange(head(grad_out, degrees), ("xh", "y"))
    plan, own = prep(tile_counts, row, tile_rows, tile_cols, features)
    z = row >> 2
    above, below = shift_z(features[None], 6), shift_z(features[None], 2)
    opposite = shift_z(above, 6)
    group, above, below, plan = lax.optimization_barrier((group, above, below, plan))
    near, away_a, away_b, near_out, away_out = sparse_product(plan, z, group, tiles[0])
    away_out, opposite, late = lax.optimization_barrier((away_out, opposite, grad_out))
    feats = join(own, above, opposite, below)
    away_a, away_b = mid_part(away_a, away_b, swap_core(away_out))
    core_part = swap_core(near_out)
    part_a, part_b = swap_z(away_a, 1), swap_z_other(away_b)
    feats_x = swap_x(feats)
    own_self = self_part(own, late)
    base, total_t = base_part(z, near, core_part, feats, feats_x)
    keep, send, kept, sent = neigh_part(core, z, base, part_a, part_b, feats, feats_x, total_t, own_self)
    kept = kept + swap_core(sent)
    got = swap_z(send, 2)
    pieces = exchange(kept.reshape(16, 16, 256), ("xh", "xl", "y"))
    pieces, keep, send = fold(1.0, pieces, 8, keep, got)
    got = swap_x(send)
    pieces = exchange(pieces, ("z",))
    pieces, keep, send = fold(1.0 / node_total, pieces, 16, keep, got)
    got = swap_z(send, 4)
    full = exchange(pieces, ("xh", "xl", "y")).reshape(256, 256)
    other = swap_core(full)
    grad_x = dense(keep, got, grad_out, w_self, w_neigh)
    grad_self, grad_neigh, grad_x = last(core, full, other, grad_x)
    return grad_x, grad_self, grad_neigh


def solution(mesh):
    in_specs = (
        P(("row", "blk"), None),
        P(("row", "blk"), None),
        P(),
        P(),
        P(("row", "blk"), None, None, None),
        P(("row", "blk"), None),
        P(("row", "blk"), None),
        P(("row", "blk")),
        P(("row", "blk")),
    )
    out_specs = (P(("row", "blk"), None), P(), P())
    return jax.shard_map(shards, mesh=mesh, in_specs=in_specs, out_specs=out_specs, check_vma=False)
```

```python
import functools
import itertools

import jax
import jax.numpy as jnp
from jax import lax
from jax.experimental import pallas as pl
from jax.experimental.pallas import tpu as pltpu
from jax.sharding import PartitionSpec as P

PARTS = {"z": 8, "xl": 2, "core": 2, "xh": 2, "y": 4}
CHUNK = 16
DEG_ROWS = 16
LARGE, SMALL = 16, 4
TRASH = 32
ZERO_ROW = 8
MIB = 1024 * 1024
DENSE_FLOPS = 5 * 10**9
SPARSE_MIB = 48
VMEM = pl.BlockSpec(memory_space=pltpu.VMEM)
SMEM = pl.BlockSpec(memory_space=pltpu.SMEM)
ANY = pl.BlockSpec(memory_space=pl.ANY)


def device_id(where):
    row = (where["z"] * 2 + where["xl"]) * 2 + where["core"]
    return row * 8 + where["xh"] * 4 + where["y"]


def groups_of(names):
    rest = [name for name in PARTS if name not in names]
    groups = []
    for fixed in itertools.product(*[range(PARTS[name]) for name in rest]):
        where = dict(zip(rest, fixed))
        group = []
        for moving in itertools.product(*[range(PARTS[name]) for name in names]):
            where.update(zip(names, moving))
            group.append(device_id(where))
        groups.append(group)
    return groups


def exchange(blocks, names):
    return lax.all_to_all(
        blocks, ("row", "blk"), 0, 0, axis_index_groups=groups_of(names), tiled=True
    )


def spread(block, names, count):
    return exchange(jnp.broadcast_to(block[None], (count,) + block.shape), names)


def swap_core(value):
    return lax.ppermute(value, "row", [(row, row ^ 1) for row in range(32)])


def params(mib):
    return pltpu.CompilerParams(vmem_limit_bytes=mib * MIB)


def head_kernel(grads, degrees, out, block, degree, sems):
    loads = [
        pltpu.make_async_copy(degrees, degree, sems.at[8]),
        pltpu.make_async_copy(grads, block.at[pl.ds(0, 128)], sems.at[9]),
    ]
    for load in loads:
        load.start()
    loads[0].wait()
    value = jnp.broadcast_to(degree[...], (DEG_ROWS, 128)).astype(jnp.float32)
    block[128 : 128 + DEG_ROWS, 0:128] = value.astype(jnp.bfloat16)
    block[128 : 128 + DEG_ROWS, 128:256] = jnp.zeros((DEG_ROWS, 128), jnp.bfloat16)
    loads[1].wait()
    stores = [pltpu.make_async_copy(block, out.at[k], sems.at[k]) for k in range(8)]
    for store in stores:
        store.start()
    for store in stores:
        store.wait()


def head(grads, degrees):
    return pl.pallas_call(
        head_kernel,
        in_specs=[ANY, ANY],
        out_specs=ANY,
        out_shape=jax.ShapeDtypeStruct((8, 128 + DEG_ROWS, 256), jnp.bfloat16),
        scratch_shapes=[
            pltpu.VMEM((128 + DEG_ROWS, 256), jnp.bfloat16),
            pltpu.VMEM((1, 128), jnp.int32),
            pltpu.SemaphoreType.DMA((10,)),
        ],
        compiler_params=params(60),
        name="head",
    )(grads, degrees[None])


def self_kernel(feats, grads, own_self):
    own_self[...] = lax.dot_general(
        feats[0], grads[...], (((0,), (0,)), ((), ())), preferred_element_type=jnp.float32
    )


def self_part(feats, grads):
    return pl.pallas_call(
        self_kernel,
        in_specs=[VMEM, VMEM],
        out_specs=VMEM,
        out_shape=jax.ShapeDtypeStruct((256, 256), jnp.float32),
        compiler_params=params(4),
        name="self",
    )(feats, grads)


def prep_kernel(counts, row, rows, cols, feats, plan, own):
    own[0] = feats[...]
    live = counts[0]
    slots = rows.shape[1]
    slot = lax.broadcasted_iota(jnp.int32, (1, slots), 1)
    lanes = lax.broadcasted_iota(jnp.int32, (8, slots), 0)
    hot = jnp.where((rows[...] == lanes) & (slot < live), 1.0, 0.0)
    earlier = lax.broadcasted_iota(jnp.int32, (slots, slots), 0) < lax.broadcasted_iota(
        jnp.int32, (slots, slots), 1
    )
    earlier = jnp.where(earlier, 1.0, 0.0).astype(jnp.bfloat16)

    def before(flags):
        return jnp.dot(flags.astype(jnp.bfloat16), earlier, preferred_element_type=jnp.float32)

    rank = jnp.sum(hot * before(hot), axis=0, keepdims=True).astype(jnp.int32)
    count = jnp.sum(hot * jnp.sum(hot, axis=1, keepdims=True), axis=0, keepdims=True)
    second = jnp.where((slot < live) & ((rank & 1) == 1), 1.0, 0.0)
    single = jnp.where((slot < live) & ((rank & 1) == 0) & (rank + 1 == count.astype(jnp.int32)), 1.0, 0.0)
    pairs = jnp.sum(second, axis=1, keepdims=True).astype(jnp.int32)
    total = pairs + jnp.sum(single, axis=1, keepdims=True).astype(jnp.int32)
    place_of_second = jnp.where(second > 0, before(jnp.broadcast_to(second, (8, slots)))[0:1], -1.0)
    place_of_single = before(jnp.broadcast_to(single, (8, slots)))[0:1].astype(jnp.int32) + pairs
    place_of_single = jnp.where(single > 0, place_of_single, -1)
    key = jnp.where(slot < live, rows[...] * 256 + (rank >> 1), -1).astype(jnp.float32)
    entry = lax.broadcasted_iota(jnp.int32, (128, slots), 0)
    is_second = jnp.where(entry == place_of_second.astype(jnp.int32), 1.0, 0.0)
    entry_key = jnp.sum(is_second * key, axis=1, keepdims=True)
    is_first = (entry < pairs) & (key == entry_key) & (second == 0)
    is_first = jnp.where(is_first | (entry == place_of_single), 1.0, 0.0)
    far = cols[...] ^ row[0]
    place = (far & 1) * 16 + (far & 4) * 2 + (far & 8) // 2 + (far & 2) + (far >> 4)
    values = jnp.where(lanes == 0, slot, 0) + jnp.where(lanes == 1, place, 0)
    values += jnp.where(lanes == 2, rows[...], 0) + jnp.where(lanes == 3, 1, 0)
    values = values.astype(jnp.float32).astype(jnp.bfloat16)

    def pick(chosen):
        nt = (((1,), (1,)), ((), ()))
        chosen = chosen.astype(jnp.bfloat16)
        return lax.dot_general(values, chosen, nt, preferred_element_type=jnp.float32).astype(jnp.int32)

    one, two = pick(is_first), pick(is_second)
    plan[0:1, :] = one[0:1]
    plan[1:2, :] = two[0:1]
    plan[2:3, :] = one[1:2] + (1 - one[3:4]) * TRASH
    plan[3:4, :] = two[1:2] + (1 - two[3:4]) * TRASH
    plan[4:5, :] = one[2:3] + (1 - one[3:4]) * ZERO_ROW
    plan[5:6, :] = jnp.broadcast_to(total, (1, 128))
    plan[6:7, :] = (jnp.maximum(one[0:1], two[0:1]) >> 4) + 1
    plan[7:8, :] = jnp.full((1, 128), (live + CHUNK - 1) >> 4, jnp.int32)


def prep(counts, row, rows, cols, feats):
    return pl.pallas_call(
        prep_kernel,
        in_specs=[SMEM, SMEM, VMEM, VMEM, VMEM],
        out_specs=[VMEM, VMEM],
        out_shape=[
            jax.ShapeDtypeStruct((8, 128), jnp.int32),
            jax.ShapeDtypeStruct((1, 128, 256), jnp.bfloat16),
        ],
        compiler_params=params(10),
        cost_estimate=pl.CostEstimate(flops=0, bytes_accessed=4 * MIB, transcendentals=0),
        name="prep",
    )(counts, row[None], rows, cols, feats)


def join_kernel(*refs):
    for k, ref in enumerate(refs[:-1]):
        refs[-1][k] = ref[0]


def join(*blocks):
    return pl.pallas_call(
        join_kernel,
        in_specs=[VMEM] * len(blocks),
        out_specs=VMEM,
        out_shape=jax.ShapeDtypeStruct((len(blocks),) + blocks[0].shape[1:], blocks[0].dtype),
        compiler_params=params(4),
        name="join",
    )(*blocks)


def sparse_kernel(plan, z, grads, tiles, near, away_a, away_b, near_out, away_out, lhs, acc, held, sems):
    chunks = plan[7, 0]

    def piece(k):
        part = pl.ds(k * CHUNK, CHUNK)
        return pltpu.make_async_copy(tiles.at[part], held.at[part], sems.at[k])

    def wait_piece(k, carry):
        piece(k).wait()
        return carry

    for k in range(192 // CHUNK):
        pl.when(k < chunks)(lambda k=k: piece(k).start())
    for k in range(8):
        grad_t = grads[k, 0:128, :].T.astype(jnp.float32)
        degree = 1.0 / grads[k, 128:129, 0:128].astype(jnp.float32)
        value = grad_t * degree
        high = value.astype(jnp.bfloat16)
        low = (value - high.astype(jnp.float32)).astype(jnp.bfloat16)
        lhs[k, :, 0:128] = high
        lhs[k, :, 128:256] = low
    lhs[ZERO_ROW] = jnp.zeros((256, 256), jnp.bfloat16)

    for k in range(32):
        acc[k] = jnp.zeros((256, 128), jnp.float32)

    def pairs(first, count, waited):
        need = waited
        for u in range(count):
            need = jnp.maximum(need, plan[6, first + u])
        lax.fori_loop(waited, need, wait_piece, 0)
        for u in range(count):
            p = first + u
            both = jnp.concatenate([held[plan[0, p]], held[plan[1, p]]], axis=1)
            product = jnp.dot(
                lhs[plan[4, p]],
                jnp.concatenate([both, both], axis=0),
                preferred_element_type=jnp.float32,
            )
            acc[plan[2, p]] += product[:, 0:128]
            acc[plan[3, p]] += product[:, 128:256]
        return need

    total = plan[5, 0]
    large = total // LARGE
    start = large * LARGE
    small = (total - start + SMALL - 1) // SMALL
    waited = lax.fori_loop(
        0, large, lambda step, waited: pairs(step * LARGE, LARGE, waited), jnp.int32(0)
    )
    waited = lax.fori_loop(
        0, small, lambda step, waited: pairs(start + step * SMALL, SMALL, waited), waited
    )
    lax.fori_loop(waited, chunks, wait_piece, 0)

    turn = 4 ^ (((z[0] + 1) >> 1) + 1 & 1)

    def move(k, carry):
        near[k] = acc[k]
        near_out[k] = acc[16 + k].astype(jnp.bfloat16)
        away_a[k] = acc[8 + k, 0:128, :]
        away_b[k] = acc[8 + (k ^ turn), 128:256, :]
        away_out[0, k] = acc[24 + k, 0:128, :].astype(jnp.bfloat16)
        away_out[1, k] = acc[24 + (k ^ turn), 128:256, :].astype(jnp.bfloat16)
        return carry

    lax.fori_loop(0, 8, move, 0)


def sparse_product(plan, z, grads, tiles):
    return pl.pallas_call(
        sparse_kernel,
        in_specs=[SMEM, SMEM, VMEM, ANY],
        out_specs=[VMEM] * 5,
        out_shape=[
            jax.ShapeDtypeStruct((8, 256, 128), jnp.float32),
            jax.ShapeDtypeStruct((8, 128, 128), jnp.float32),
            jax.ShapeDtypeStruct((8, 128, 128), jnp.float32),
            jax.ShapeDtypeStruct((8, 256, 128), jnp.bfloat16),
            jax.ShapeDtypeStruct((2, 8, 128, 128), jnp.bfloat16),
        ],
        scratch_shapes=[
            pltpu.VMEM((9, 256, 256), jnp.bfloat16),
            pltpu.VMEM((33, 256, 128), jnp.float32),
            pltpu.VMEM((192, 128, 128), jnp.bfloat16),
            pltpu.SemaphoreType.DMA((192 // CHUNK,)),
        ],
        compiler_params=params(SPARSE_MIB),
        cost_estimate=pl.CostEstimate(flops=4 * 10**9, bytes_accessed=12 * MIB, transcendentals=0),
        name="sparse",
    )(plan, z[None], grads, tiles)


def mid_kernel(away_a, away_b, part, out_a, out_b):
    for k in range(8):
        out_a[k] = (away_a[k] + part[0, k].astype(jnp.float32)).astype(jnp.bfloat16)
        out_b[k] = (away_b[k] + part[1, k].astype(jnp.float32)).astype(jnp.bfloat16)


def mid_part(away_a, away_b, part):
    return pl.pallas_call(
        mid_kernel,
        in_specs=[VMEM] * 3,
        out_specs=[VMEM] * 2,
        out_shape=[jax.ShapeDtypeStruct((8, 128, 128), jnp.bfloat16)] * 2,
        compiler_params=params(8),
        name="mid",
    )(away_a, away_b, part)


def feat_of(z, low, high, k):
    turn = z[0] & 2
    place = [0, 1 + turn, 2, 3 - turn][(k & 1) * 2 + (k >> 2)]
    return (high if k & 2 else low)[place]


def base_kernel(z, near, core_part, feats_low, feats_high, base, total_t):
    total = jnp.zeros((256, 256), jnp.float32)
    for k in range(8):
        block = near[k] + core_part[k].astype(jnp.float32)
        base[k] = block
        high = block.astype(jnp.bfloat16)
        low = (block - high.astype(jnp.float32)).astype(jnp.bfloat16)
        feat = feat_of(z, feats_low, feats_high, k)
        total += jnp.dot(
            jnp.concatenate([high, low], axis=1),
            jnp.concatenate([feat, feat], axis=0),
            preferred_element_type=jnp.float32,
        )
    total_t[...] = total


def base_part(z, near, core_part, feats_low, feats_high):
    return pl.pallas_call(
        base_kernel,
        in_specs=[SMEM] + [VMEM] * 4,
        out_specs=[VMEM] * 2,
        out_shape=[
            jax.ShapeDtypeStruct((8, 256, 128), jnp.float32),
            jax.ShapeDtypeStruct((256, 256), jnp.float32),
        ],
        compiler_params=params(12),
        cost_estimate=pl.CostEstimate(flops=10**9, bytes_accessed=4 * MIB, transcendentals=0),
        name="base",
    )(z[None], near, core_part, feats_low, feats_high)


def neigh_kernel(core, z, base, part_a, part_b, feats_low, feats_high, total_t, own_self, keep, send, kept, sent):
    total = total_t[...]
    z_part = [jnp.concatenate([part_a[k], part_b[k]], axis=0) for k in range(8)]
    for k in range(0, 8, 2):
        pair = [feat_of(z, feats_low, feats_high, k + u) for u in range(2)]
        total += jnp.dot(
            jnp.concatenate([z_part[k], z_part[k + 1]], axis=1),
            jnp.concatenate(pair, axis=0),
            preferred_element_type=jnp.float32,
        )
    total = total.T
    for k in range(8):
        block = base[k] + z_part[k].astype(jnp.float32)
        if k < 4:
            keep[k] = block
        else:
            send[k - 4] = block.astype(jnp.bfloat16)
    first = core[0] == 0

    @pl.when(first)
    def _():
        kept[...] = own_self[...]
        sent[...] = total

    @pl.when(jnp.logical_not(first))
    def _():
        kept[...] = total
        sent[...] = own_self[...]


def neigh_part(core, z, base, part_a, part_b, feats_low, feats_high, total_t, own_self):
    return pl.pallas_call(
        neigh_kernel,
        in_specs=[SMEM] * 2 + [VMEM] * 7,
        out_specs=[VMEM] * 4,
        out_shape=[
            jax.ShapeDtypeStruct((4, 256, 128), jnp.float32),
            jax.ShapeDtypeStruct((4, 256, 128), jnp.bfloat16),
            jax.ShapeDtypeStruct((256, 256), jnp.float32),
            jax.ShapeDtypeStruct((256, 256), jnp.float32),
        ],
        compiler_params=params(12),
        cost_estimate=pl.CostEstimate(flops=10**9, bytes_accessed=4 * MIB, transcendentals=0),
        name="neigh",
    )(core[None], z[None], base, part_a, part_b, feats_low, feats_high, total_t, own_self)


def fold_kernel(scale, pieces, keep, got, out, *rest):
    total = pieces[0]
    for k in range(1, pieces.shape[0]):
        total += pieces[k]
    total = total * scale
    for k in range(out.shape[0]):
        out[k] = total
    half = keep.shape[0] // 2
    kept, send = rest
    for k in range(half):
        kept[k] = keep[k] + got[k].astype(jnp.float32)
        send[k] = (keep[half + k] + got[half + k].astype(jnp.float32)).astype(jnp.bfloat16)


def fold(scale, pieces, receivers, keep, got):
    half = keep.shape[0] // 2
    return pl.pallas_call(
        functools.partial(fold_kernel, scale),
        in_specs=[VMEM] * 3,
        out_specs=[VMEM] * 3,
        out_shape=[
            jax.ShapeDtypeStruct((receivers, 16, 256), jnp.float32),
            jax.ShapeDtypeStruct((half, 256, 128), jnp.float32),
            jax.ShapeDtypeStruct((half, 256, 128), jnp.bfloat16),
        ],
        compiler_params=params(8),
        name="fold",
    )(pieces, keep, got)


def dense_kernel(own, part, grads, w_self, w_neigh, grad_x):
    total = own[0] + part[0].astype(jnp.float32)
    high = total.astype(jnp.bfloat16)
    low = (total - high.astype(jnp.float32)).astype(jnp.bfloat16)
    nt = (((1,), (1,)), ((), ()))
    out = lax.dot_general(w_self[...], grads[...], nt, preferred_element_type=jnp.float32)
    out += jnp.dot(w_neigh[...], high, preferred_element_type=jnp.float32)
    out += jnp.dot(w_neigh[...], low, preferred_element_type=jnp.float32)
    grad_x[...] = out.T.astype(jnp.bfloat16)


def dense(own, part, grads, w_self, w_neigh):
    return pl.pallas_call(
        dense_kernel,
        in_specs=[VMEM] * 5,
        out_specs=VMEM,
        out_shape=jax.ShapeDtypeStruct((128, 256), jnp.bfloat16),
        compiler_params=params(8),
        cost_estimate=pl.CostEstimate(flops=DENSE_FLOPS, bytes_accessed=MIB, transcendentals=0),
        name="dense",
    )(own, part, grads, w_self, w_neigh)


def last_kernel(core, full, other, done_x, grad_self, grad_neigh, grad_x):
    first = core[0] == 0
    grad_x[...] = done_x[...]

    @pl.when(first)
    def _():
        grad_self[...] = full[...]
        grad_neigh[...] = other[...]

    @pl.when(jnp.logical_not(first))
    def _():
        grad_self[...] = other[...]
        grad_neigh[...] = full[...]


def last(core, full, other, done_x):
    return pl.pallas_call(
        last_kernel,
        in_specs=[SMEM] + [VMEM] * 3,
        out_specs=[VMEM] * 3,
        out_shape=[
            jax.ShapeDtypeStruct((256, 256), jnp.float32),
            jax.ShapeDtypeStruct((256, 256), jnp.float32),
            jax.ShapeDtypeStruct((128, 256), jnp.bfloat16),
        ],
        compiler_params=params(8),
        name="last",
    )(core[None], full, other, done_x)


def swap_z(value, distance):
    return lax.ppermute(value, "row", [(row, row ^ (4 * distance)) for row in range(32)])


def shift_z(value, steps):
    pairs = [(row, (row + 4 * steps) % 32) for row in range(32)]
    return lax.ppermute(value, "row", pairs)


def swap_z_other(value):
    pairs = []
    for row in range(32):
        z = row >> 2
        other = (z + 1) % 8 if z & 1 else (z - 1) % 8
        pairs.append((row, other * 4 + (row & 3)))
    return lax.ppermute(value, "row", pairs)


def swap_x(value):
    return lax.ppermute(value, "row", [(row, row ^ 2) for row in range(32)])


def shards(features, grad_out, w_self, w_neigh, tiles, tile_rows, tile_cols, tile_counts, degrees):
    row = lax.axis_index("row").astype(jnp.int32)
    core = row & 1
    node_total = 128 * 256
    group = exchange(head(grad_out, degrees), ("xh", "y"))
    plan, own = prep(tile_counts, row, tile_rows, tile_cols, features)
    z = row >> 2
    above, below = shift_z(features[None], 6), shift_z(features[None], 2)
    opposite = shift_z(above, 6)
    group, above, below, plan = lax.optimization_barrier((group, above, below, plan))
    near, away_a, away_b, near_out, away_out = sparse_product(plan, z, group, tiles[0])
    away_out, opposite, late = lax.optimization_barrier((away_out, opposite, grad_out))
    feats = join(own, above, opposite, below)
    away_a, away_b = mid_part(away_a, away_b, swap_core(away_out))
    core_part = swap_core(near_out)
    part_a, part_b = swap_z(away_a, 1), swap_z_other(away_b)
    feats_x = swap_x(feats)
    own_self = self_part(own, late)
    base, total_t = base_part(z, near, core_part, feats, feats_x)
    keep, send, kept, sent = neigh_part(core, z, base, part_a, part_b, feats, feats_x, total_t, own_self)
    kept = kept + swap_core(sent)
    got = swap_z(send, 2)
    pieces = exchange(kept.reshape(16, 16, 256), ("xh", "xl", "y"))
    pieces, keep, send = fold(1.0, pieces, 8, keep, got)
    got = swap_x(send)
    pieces = exchange(pieces, ("z",))
    pieces, keep, send = fold(1.0 / node_total, pieces, 16, keep, got)
    got = swap_z(send, 4)
    full = exchange(pieces, ("xh", "xl", "y")).reshape(256, 256)
    other = swap_core(full)
    grad_x = dense(keep, got, grad_out, w_self, w_neigh)
    grad_self, grad_neigh, grad_x = last(core, full, other, grad_x)
    return grad_x, grad_self, grad_neigh


def solution(mesh):
    in_specs = (
        P(("row", "blk"), None),
        P(("row", "blk"), None),
        P(),
        P(),
        P(("row", "blk"), None, None, None),
        P(("row", "blk"), None),
        P(("row", "blk"), None),
        P(("row", "blk")),
        P(("row", "blk")),
    )
    out_specs = (P(("row", "blk"), None), P(), P())
    return jax.shard_map(shards, mesh=mesh, in_specs=in_specs, out_specs=out_specs, check_vma=False)
```

```python
import functools
import itertools

import jax
import jax.numpy as jnp
from jax import lax
from jax.experimental import pallas as pl
from jax.experimental.pallas import tpu as pltpu
from jax.sharding import PartitionSpec as P

PARTS = {"z": 8, "xl": 2, "core": 2, "xh": 2, "y": 4}
CHUNK = 16
DEG_ROWS = 16
LARGE, SMALL = 16, 4
TRASH = 32
ZERO_ROW = 8
MIB = 1024 * 1024
DENSE_FLOPS = 5 * 10**9
SPARSE_MIB = 48
VMEM = pl.BlockSpec(memory_space=pltpu.VMEM)
SMEM = pl.BlockSpec(memory_space=pltpu.SMEM)
ANY = pl.BlockSpec(memory_space=pl.ANY)


def device_id(where):
    row = (where["z"] * 2 + where["xl"]) * 2 + where["core"]
    return row * 8 + where["xh"] * 4 + where["y"]


def groups_of(names):
    rest = [name for name in PARTS if name not in names]
    groups = []
    for fixed in itertools.product(*[range(PARTS[name]) for name in rest]):
        where = dict(zip(rest, fixed))
        group = []
        for moving in itertools.product(*[range(PARTS[name]) for name in names]):
            where.update(zip(names, moving))
            group.append(device_id(where))
        groups.append(group)
    return groups


def exchange(blocks, names):
    return lax.all_to_all(
        blocks, ("row", "blk"), 0, 0, axis_index_groups=groups_of(names), tiled=True
    )


def spread(block, names, count):
    return exchange(jnp.broadcast_to(block[None], (count,) + block.shape), names)


def swap_core(value):
    return lax.ppermute(value, "row", [(row, row ^ 1) for row in range(32)])


def params(mib):
    return pltpu.CompilerParams(vmem_limit_bytes=mib * MIB)


def head_kernel(grads, degrees, out, block, degree, sems):
    loads = [
        pltpu.make_async_copy(degrees, degree, sems.at[8]),
        pltpu.make_async_copy(grads, block.at[pl.ds(0, 128)], sems.at[9]),
    ]
    for load in loads:
        load.start()
    loads[0].wait()
    value = jnp.broadcast_to(degree[...], (DEG_ROWS, 128)).astype(jnp.float32)
    block[128 : 128 + DEG_ROWS, 0:128] = value.astype(jnp.bfloat16)
    block[128 : 128 + DEG_ROWS, 128:256] = jnp.zeros((DEG_ROWS, 128), jnp.bfloat16)
    loads[1].wait()
    stores = [pltpu.make_async_copy(block, out.at[k], sems.at[k]) for k in range(8)]
    for store in stores:
        store.start()
    for store in stores:
        store.wait()


def head(grads, degrees):
    return pl.pallas_call(
        head_kernel,
        in_specs=[ANY, ANY],
        out_specs=ANY,
        out_shape=jax.ShapeDtypeStruct((8, 128 + DEG_ROWS, 256), jnp.bfloat16),
        scratch_shapes=[
            pltpu.VMEM((128 + DEG_ROWS, 256), jnp.bfloat16),
            pltpu.VMEM((1, 128), jnp.int32),
            pltpu.SemaphoreType.DMA((10,)),
        ],
        compiler_params=params(60),
        name="head",
    )(grads, degrees[None])


def self_kernel(feats, grads, own_self):
    own_self[...] = lax.dot_general(
        feats[0], grads[...], (((0,), (0,)), ((), ())), preferred_element_type=jnp.float32
    )


def self_part(feats, grads):
    return pl.pallas_call(
        self_kernel,
        in_specs=[VMEM, VMEM],
        out_specs=VMEM,
        out_shape=jax.ShapeDtypeStruct((256, 256), jnp.float32),
        compiler_params=params(4),
        name="self",
    )(feats, grads)


def prep_kernel(counts, row, rows, cols, feats, plan, own):
    own[0] = feats[...]
    live = counts[0]
    slots = rows.shape[1]
    slot = lax.broadcasted_iota(jnp.int32, (1, slots), 1)
    lanes = lax.broadcasted_iota(jnp.int32, (8, slots), 0)
    hot = jnp.where((rows[...] == lanes) & (slot < live), 1.0, 0.0)
    earlier = lax.broadcasted_iota(jnp.int32, (slots, slots), 0) < lax.broadcasted_iota(
        jnp.int32, (slots, slots), 1
    )
    earlier = jnp.where(earlier, 1.0, 0.0).astype(jnp.bfloat16)

    def before(flags):
        return jnp.dot(flags.astype(jnp.bfloat16), earlier, preferred_element_type=jnp.float32)

    rank = jnp.sum(hot * before(hot), axis=0, keepdims=True).astype(jnp.int32)
    count = jnp.sum(hot * jnp.sum(hot, axis=1, keepdims=True), axis=0, keepdims=True)
    second = jnp.where((slot < live) & ((rank & 1) == 1), 1.0, 0.0)
    single = jnp.where((slot < live) & ((rank & 1) == 0) & (rank + 1 == count.astype(jnp.int32)), 1.0, 0.0)
    pairs = jnp.sum(second, axis=1, keepdims=True).astype(jnp.int32)
    total = pairs + jnp.sum(single, axis=1, keepdims=True).astype(jnp.int32)
    place_of_second = jnp.where(second > 0, before(jnp.broadcast_to(second, (8, slots)))[0:1], -1.0)
    place_of_single = before(jnp.broadcast_to(single, (8, slots)))[0:1].astype(jnp.int32) + pairs
    place_of_single = jnp.where(single > 0, place_of_single, -1)
    key = jnp.where(slot < live, rows[...] * 256 + (rank >> 1), -1).astype(jnp.float32)
    entry = lax.broadcasted_iota(jnp.int32, (128, slots), 0)
    is_second = jnp.where(entry == place_of_second.astype(jnp.int32), 1.0, 0.0)
    entry_key = jnp.sum(is_second * key, axis=1, keepdims=True)
    is_first = (entry < pairs) & (key == entry_key) & (second == 0)
    is_first = jnp.where(is_first | (entry == place_of_single), 1.0, 0.0)
    far = cols[...] ^ row[0]
    place = (far & 1) * 16 + (far & 4) * 2 + (far & 8) // 2 + (far & 2) + (far >> 4)
    values = jnp.where(lanes == 0, slot, 0) + jnp.where(lanes == 1, place, 0)
    values += jnp.where(lanes == 2, rows[...], 0) + jnp.where(lanes == 3, 1, 0)
    values = values.astype(jnp.float32).astype(jnp.bfloat16)

    def pick(chosen):
        nt = (((1,), (1,)), ((), ()))
        chosen = chosen.astype(jnp.bfloat16)
        return lax.dot_general(values, chosen, nt, preferred_element_type=jnp.float32).astype(jnp.int32)

    one, two = pick(is_first), pick(is_second)
    plan[0:1, :] = one[0:1]
    plan[1:2, :] = two[0:1]
    plan[2:3, :] = one[1:2] + (1 - one[3:4]) * TRASH
    plan[3:4, :] = two[1:2] + (1 - two[3:4]) * TRASH
    plan[4:5, :] = one[2:3] + (1 - one[3:4]) * ZERO_ROW
    plan[5:6, :] = jnp.broadcast_to(total, (1, 128))
    plan[6:7, :] = (jnp.maximum(one[0:1], two[0:1]) >> 4) + 1
    plan[7:8, :] = jnp.full((1, 128), (live + CHUNK - 1) >> 4, jnp.int32)


def prep(counts, row, rows, cols, feats):
    return pl.pallas_call(
        prep_kernel,
        in_specs=[SMEM, SMEM, VMEM, VMEM, VMEM],
        out_specs=[VMEM, VMEM],
        out_shape=[
            jax.ShapeDtypeStruct((8, 128), jnp.int32),
            jax.ShapeDtypeStruct((1, 128, 256), jnp.bfloat16),
        ],
        compiler_params=params(10),
        cost_estimate=pl.CostEstimate(flops=0, bytes_accessed=4 * MIB, transcendentals=0),
        name="prep",
    )(counts, row[None], rows, cols, feats)


def join_kernel(*refs):
    for k, ref in enumerate(refs[:-1]):
        refs[-1][k] = ref[0]


def join(*blocks):
    return pl.pallas_call(
        join_kernel,
        in_specs=[VMEM] * len(blocks),
        out_specs=VMEM,
        out_shape=jax.ShapeDtypeStruct((len(blocks),) + blocks[0].shape[1:], blocks[0].dtype),
        compiler_params=params(4),
        name="join",
    )(*blocks)


def sparse_kernel(plan, z, grads, tiles, near, away_a, away_b, near_out, away_out, lhs, acc, held, sems):
    chunks = plan[7, 0]

    def piece(k):
        part = pl.ds(k * CHUNK, CHUNK)
        return pltpu.make_async_copy(tiles.at[part], held.at[part], sems.at[k])

    def wait_piece(k, carry):
        piece(k).wait()
        return carry

    for k in range(192 // CHUNK):
        pl.when(k < chunks)(lambda k=k: piece(k).start())
    for k in range(8):
        grad_t = grads[k, 0:128, :].T.astype(jnp.float32)
        degree = 1.0 / grads[k, 128:129, 0:128].astype(jnp.float32)
        value = grad_t * degree
        high = value.astype(jnp.bfloat16)
        low = (value - high.astype(jnp.float32)).astype(jnp.bfloat16)
        lhs[k, :, 0:128] = high
        lhs[k, :, 128:256] = low
    lhs[ZERO_ROW] = jnp.zeros((256, 256), jnp.bfloat16)

    for k in range(32):
        acc[k] = jnp.zeros((256, 128), jnp.float32)

    def pairs(first, count, waited):
        need = waited
        for u in range(count):
            need = jnp.maximum(need, plan[6, first + u])
        lax.fori_loop(waited, need, wait_piece, 0)
        for u in range(count):
            p = first + u
            both = jnp.concatenate([held[plan[0, p]], held[plan[1, p]]], axis=1)
            product = jnp.dot(
                lhs[plan[4, p]],
                jnp.concatenate([both, both], axis=0),
                preferred_element_type=jnp.float32,
            )
            acc[plan[2, p]] += product[:, 0:128]
            acc[plan[3, p]] += product[:, 128:256]
        return need

    total = plan[5, 0]
    large = total // LARGE
    start = large * LARGE
    small = (total - start + SMALL - 1) // SMALL
    waited = lax.fori_loop(
        0, large, lambda step, waited: pairs(step * LARGE, LARGE, waited), jnp.int32(0)
    )
    waited = lax.fori_loop(
        0, small, lambda step, waited: pairs(start + step * SMALL, SMALL, waited), waited
    )
    lax.fori_loop(waited, chunks, wait_piece, 0)

    turn = 4 ^ (((z[0] + 1) >> 1) + 1 & 1)

    def move(k, carry):
        near[k] = acc[k]
        near_out[k] = acc[16 + k].astype(jnp.bfloat16)
        away_a[k] = acc[8 + k, 0:128, :]
        away_b[k] = acc[8 + (k ^ turn), 128:256, :]
        away_out[0, k] = acc[24 + k, 0:128, :].astype(jnp.bfloat16)
        away_out[1, k] = acc[24 + (k ^ turn), 128:256, :].astype(jnp.bfloat16)
        return carry

    lax.fori_loop(0, 8, move, 0)


def sparse_product(plan, z, grads, tiles):
    return pl.pallas_call(
        sparse_kernel,
        in_specs=[SMEM, SMEM, VMEM, ANY],
        out_specs=[VMEM] * 5,
        out_shape=[
            jax.ShapeDtypeStruct((8, 256, 128), jnp.float32),
            jax.ShapeDtypeStruct((8, 128, 128), jnp.float32),
            jax.ShapeDtypeStruct((8, 128, 128), jnp.float32),
            jax.ShapeDtypeStruct((8, 256, 128), jnp.bfloat16),
            jax.ShapeDtypeStruct((2, 8, 128, 128), jnp.bfloat16),
        ],
        scratch_shapes=[
            pltpu.VMEM((9, 256, 256), jnp.bfloat16),
            pltpu.VMEM((33, 256, 128), jnp.float32),
            pltpu.VMEM((192, 128, 128), jnp.bfloat16),
            pltpu.SemaphoreType.DMA((192 // CHUNK,)),
        ],
        compiler_params=params(SPARSE_MIB),
        cost_estimate=pl.CostEstimate(flops=4 * 10**9, bytes_accessed=12 * MIB, transcendentals=0),
        name="sparse",
    )(plan, z[None], grads, tiles)


def mid_kernel(away_a, away_b, part, out_a, out_b):
    for k in range(8):
        out_a[k] = (away_a[k] + part[0, k].astype(jnp.float32)).astype(jnp.bfloat16)
        out_b[k] = (away_b[k] + part[1, k].astype(jnp.float32)).astype(jnp.bfloat16)


def mid_part(away_a, away_b, part):
    return pl.pallas_call(
        mid_kernel,
        in_specs=[VMEM] * 3,
        out_specs=[VMEM] * 2,
        out_shape=[jax.ShapeDtypeStruct((8, 128, 128), jnp.bfloat16)] * 2,
        compiler_params=params(8),
        name="mid",
    )(away_a, away_b, part)


def feat_of(z, low, high, k):
    turn = z[0] & 2
    place = [0, 1 + turn, 2, 3 - turn][(k & 1) * 2 + (k >> 2)]
    return (high if k & 2 else low)[place]


def base_kernel(z, near, core_part, feats_low, feats_high, base, total_t):
    total = jnp.zeros((256, 256), jnp.float32)
    for k in range(8):
        block = near[k] + core_part[k].astype(jnp.float32)
        base[k] = block
        high = block.astype(jnp.bfloat16)
        low = (block - high.astype(jnp.float32)).astype(jnp.bfloat16)
        feat = feat_of(z, feats_low, feats_high, k)
        total += jnp.dot(
            jnp.concatenate([high, low], axis=1),
            jnp.concatenate([feat, feat], axis=0),
            preferred_element_type=jnp.float32,
        )
    total_t[...] = total


def base_part(z, near, core_part, feats_low, feats_high):
    return pl.pallas_call(
        base_kernel,
        in_specs=[SMEM] + [VMEM] * 4,
        out_specs=[VMEM] * 2,
        out_shape=[
            jax.ShapeDtypeStruct((8, 256, 128), jnp.float32),
            jax.ShapeDtypeStruct((256, 256), jnp.float32),
        ],
        compiler_params=params(12),
        cost_estimate=pl.CostEstimate(flops=10**9, bytes_accessed=4 * MIB, transcendentals=0),
        name="base",
    )(z[None], near, core_part, feats_low, feats_high)


def neigh_kernel(core, z, base, part_a, part_b, feats_low, feats_high, total_t, own_self, keep, send, kept, sent):
    total = total_t[...]
    z_part = [jnp.concatenate([part_a[k], part_b[k]], axis=0) for k in range(8)]
    for k in range(0, 8, 2):
        pair = [feat_of(z, feats_low, feats_high, k + u) for u in range(2)]
        total += jnp.dot(
            jnp.concatenate([z_part[k], z_part[k + 1]], axis=1),
            jnp.concatenate(pair, axis=0),
            preferred_element_type=jnp.float32,
        )
    total = total.T
    for k in range(8):
        block = base[k] + z_part[k].astype(jnp.float32)
        if k < 4:
            keep[k] = block
        else:
            send[k - 4] = block.astype(jnp.bfloat16)
    first = core[0] == 0

    @pl.when(first)
    def _():
        kept[...] = own_self[...]
        sent[...] = total

    @pl.when(jnp.logical_not(first))
    def _():
        kept[...] = total
        sent[...] = own_self[...]


def neigh_part(core, z, base, part_a, part_b, feats_low, feats_high, total_t, own_self):
    return pl.pallas_call(
        neigh_kernel,
        in_specs=[SMEM] * 2 + [VMEM] * 7,
        out_specs=[VMEM] * 4,
        out_shape=[
            jax.ShapeDtypeStruct((4, 256, 128), jnp.float32),
            jax.ShapeDtypeStruct((4, 256, 128), jnp.bfloat16),
            jax.ShapeDtypeStruct((256, 256), jnp.float32),
            jax.ShapeDtypeStruct((256, 256), jnp.float32),
        ],
        compiler_params=params(12),
        cost_estimate=pl.CostEstimate(flops=10**9, bytes_accessed=4 * MIB, transcendentals=0),
        name="neigh",
    )(core[None], z[None], base, part_a, part_b, feats_low, feats_high, total_t, own_self)


def fold_kernel(scale, pieces, keep, got, out, kept, send, whole, sems):
    total = pieces[0]
    for k in range(1, pieces.shape[0]):
        total += pieces[k]
    whole[...] = total * scale
    copies = [pltpu.make_async_copy(whole, out.at[k], sems.at[k]) for k in range(out.shape[0])]
    for copy in copies:
        copy.start()
    half = keep.shape[0] // 2
    for k in range(half):
        kept[k] = keep[k] + got[k].astype(jnp.float32)
        send[k] = (keep[half + k] + got[half + k].astype(jnp.float32)).astype(jnp.bfloat16)
    for copy in copies:
        copy.wait()


def fold(scale, pieces, receivers, keep, got):
    half = keep.shape[0] // 2
    return pl.pallas_call(
        functools.partial(fold_kernel, scale),
        in_specs=[VMEM] * 3,
        out_specs=[ANY, VMEM, VMEM],
        out_shape=[
            jax.ShapeDtypeStruct((receivers, 16, 256), jnp.float32),
            jax.ShapeDtypeStruct((half, 256, 128), jnp.float32),
            jax.ShapeDtypeStruct((half, 256, 128), jnp.bfloat16),
        ],
        scratch_shapes=[
            pltpu.VMEM((16, 256), jnp.float32),
            pltpu.SemaphoreType.DMA((receivers,)),
        ],
        compiler_params=params(8),
        name="fold",
    )(pieces, keep, got)


def dense_kernel(own, part, grads, w_self, w_neigh, grad_x):
    total = own[0] + part[0].astype(jnp.float32)
    high = total.astype(jnp.bfloat16)
    low = (total - high.astype(jnp.float32)).astype(jnp.bfloat16)
    nt = (((1,), (1,)), ((), ()))
    out = lax.dot_general(w_self[...], grads[...], nt, preferred_element_type=jnp.float32)
    out += jnp.dot(w_neigh[...], high, preferred_element_type=jnp.float32)
    out += jnp.dot(w_neigh[...], low, preferred_element_type=jnp.float32)
    grad_x[...] = out.T.astype(jnp.bfloat16)


def dense(own, part, grads, w_self, w_neigh):
    return pl.pallas_call(
        dense_kernel,
        in_specs=[VMEM] * 5,
        out_specs=VMEM,
        out_shape=jax.ShapeDtypeStruct((128, 256), jnp.bfloat16),
        compiler_params=params(8),
        cost_estimate=pl.CostEstimate(flops=DENSE_FLOPS, bytes_accessed=MIB, transcendentals=0),
        name="dense",
    )(own, part, grads, w_self, w_neigh)


def last_kernel(core, full, other, done_x, grad_self, grad_neigh, grad_x):
    first = core[0] == 0
    grad_x[...] = done_x[...]

    @pl.when(first)
    def _():
        grad_self[...] = full[...]
        grad_neigh[...] = other[...]

    @pl.when(jnp.logical_not(first))
    def _():
        grad_self[...] = other[...]
        grad_neigh[...] = full[...]


def last(core, full, other, done_x):
    return pl.pallas_call(
        last_kernel,
        in_specs=[SMEM] + [VMEM] * 3,
        out_specs=[VMEM] * 3,
        out_shape=[
            jax.ShapeDtypeStruct((256, 256), jnp.float32),
            jax.ShapeDtypeStruct((256, 256), jnp.float32),
            jax.ShapeDtypeStruct((128, 256), jnp.bfloat16),
        ],
        compiler_params=params(8),
        name="last",
    )(core[None], full, other, done_x)


def swap_z(value, distance):
    return lax.ppermute(value, "row", [(row, row ^ (4 * distance)) for row in range(32)])


def shift_z(value, steps):
    pairs = [(row, (row + 4 * steps) % 32) for row in range(32)]
    return lax.ppermute(value, "row", pairs)


def swap_z_other(value):
    pairs = []
    for row in range(32):
        z = row >> 2
        other = (z + 1) % 8 if z & 1 else (z - 1) % 8
        pairs.append((row, other * 4 + (row & 3)))
    return lax.ppermute(value, "row", pairs)


def swap_x(value):
    return lax.ppermute(value, "row", [(row, row ^ 2) for row in range(32)])


def shards(features, grad_out, w_self, w_neigh, tiles, tile_rows, tile_cols, tile_counts, degrees):
    row = lax.axis_index("row").astype(jnp.int32)
    core = row & 1
    node_total = 128 * 256
    group = exchange(head(grad_out, degrees), ("xh", "y"))
    plan, own = prep(tile_counts, row, tile_rows, tile_cols, features)
    z = row >> 2
    above, below = shift_z(features[None], 6), shift_z(features[None], 2)
    opposite = shift_z(above, 6)
    group, above, below, plan = lax.optimization_barrier((group, above, below, plan))
    near, away_a, away_b, near_out, away_out = sparse_product(plan, z, group, tiles[0])
    away_out, opposite, late = lax.optimization_barrier((away_out, opposite, grad_out))
    feats = join(own, above, opposite, below)
    away_a, away_b = mid_part(away_a, away_b, swap_core(away_out))
    core_part = swap_core(near_out)
    part_a, part_b = swap_z(away_a, 1), swap_z_other(away_b)
    feats_x = swap_x(feats)
    own_self = self_part(own, late)
    base, total_t = base_part(z, near, core_part, feats, feats_x)
    keep, send, kept, sent = neigh_part(core, z, base, part_a, part_b, feats, feats_x, total_t, own_self)
    kept = kept + swap_core(sent)
    got = swap_z(send, 2)
    pieces = exchange(kept.reshape(16, 16, 256), ("xh", "xl", "y"))
    pieces, keep, send = fold(1.0, pieces, 8, keep, got)
    got = swap_x(send)
    pieces = exchange(pieces, ("z",))
    pieces, keep, send = fold(1.0 / node_total, pieces, 16, keep, got)
    got = swap_z(send, 4)
    full = exchange(pieces, ("xh", "xl", "y")).reshape(256, 256)
    other = swap_core(full)
    grad_x = dense(keep, got, grad_out, w_self, w_neigh)
    grad_self, grad_neigh, grad_x = last(core, full, other, grad_x)
    return grad_x, grad_self, grad_neigh


def solution(mesh):
    in_specs = (
        P(("row", "blk"), None),
        P(("row", "blk"), None),
        P(),
        P(),
        P(("row", "blk"), None, None, None),
        P(("row", "blk"), None),
        P(("row", "blk"), None),
        P(("row", "blk")),
        P(("row", "blk")),
    )
    out_specs = (P(("row", "blk"), None), P(), P())
    return jax.shard_map(shards, mesh=mesh, in_specs=in_specs, out_specs=out_specs, check_vma=False)
```
